128 devices in a mesh: seq: 8 (over z, x_hi), shard: 16 (over y, x_lo, core).
Axes of the slice: x: 4 (x_hi: 2, x_lo: 2; x = x_hi * 2 + x_lo), y: 4, z: 4, core: 2. Of those that a mesh axis runs over, the one named last changes fastest.
Arguments:
- tokens: bfloat16 [16, 1024, 1536], P('shard', 'seq'), may hold values from -6 to 6
- lengths: int32 [16], P('shard'), may hold values from 256 to 1024, as said below
- cotangent: bfloat16 [16, 1024, 1536], P('shard', 'seq'), may hold values from -6 to 6
- gain_one: bfloat16 [1536], P('shard'), may hold values from 0.099609375 to 1.8984375
- in_weight: bfloat16 [1536, 4608], P('shard'), may hold values from -0.15625 to 0.15625
- conv_weight: bfloat16 [3, 1536], P(None, 'shard'), may hold values from -3 to 3
- out_weight: bfloat16 [1536, 1536], P('shard'), may hold values from -0.15625 to 0.15625
- gain_two: bfloat16 [1536], P('shard'), may hold values from 0.099609375 to 1.8984375
- gate_weight: bfloat16 [1536, 6912], P('shard'), may hold values from -0.15625 to 0.15625
- up_weight: bfloat16 [1536, 6912], P('shard'), may hold values from -0.15625 to 0.15625
- down_weight: bfloat16 [6912, 1536], P('shard'), may hold values from -0.078125 to 0.078125
Outputs:
- output: bfloat16 [16, 1024, 1536], P('shard', 'seq')
- grad_tokens: float32 [16, 1024, 1536], P('shard', 'seq')
- grad_gain_one: float32 [1536], P('shard')
- grad_in_weight: float32 [1536, 4608], P('shard')
- grad_conv_weight: float32 [3, 1536], P(None, 'shard')
- grad_out_weight: float32 [1536, 1536], P('shard')
- grad_gain_two: float32 [1536], P('shard')
- grad_gate_weight: float32 [1536, 6912], P('shard')
- grad_up_weight: float32 [1536, 6912], P('shard')
- grad_down_weight: float32 [6912, 1536], P('shard')
The draws below stay inside these ranges and needn't reach their ends.
Inputs may be any that keep to these rules, and one draw needn't show every extreme that they name: `lengths`: in each aligned pair of sequences (0 and 1, 2 and 3, and so on) one, drawn from the seed, has length 1024.
All inputs are finite; a program needn't handle non-finite values.
Results may differ from the reference program's by a relative error of at most 0.022.
Values may be sent and summed in bfloat16 or wider, within the bound.
No kernel may reach another device: no remote copies, remote signals or barrier semaphores. Data moves between devices by JAX's collectives and lax.ppermute only.
A program may use at most 320 MiB of HBM per device.

```python
import jax
import jax.numpy as jnp
from jax import lax

D = 1536
FF = 6912
SLOTS = 1024
SEQS = 16


def draw_lengths(key, part):
    key = jax.random.fold_in(key, 7)
    pick_key, length_key = jax.random.split(key)
    pairs = SEQS // 2
    full_side = jax.random.randint(pick_key, (pairs,), 0, 2)
    drawn = jax.random.randint(length_key, (pairs, 2), SLOTS // 4, SLOTS + 1)
    sides = jnp.arange(2, dtype=jnp.int32)
    chosen = jnp.where(sides[None, :] == full_side[:, None], SLOTS, drawn)
    return chosen.reshape(SEQS).astype(jnp.int32)


def block_levels(own_key, dims, pieces, low, high):
    def one(dim, parts):
        steps = jax.random.uniform(jax.random.fold_in(jax.random.fold_in(own_key, 6), dim), (parts,), jnp.float32, low / len(pieces), high / len(pieces))
        return jnp.repeat(jnp.exp(steps), dims[dim] // parts).reshape((-1,) + (1,) * (len(dims) - dim - 1))

    level = one(*pieces[0])
    for cut in pieces[1:]:
        level = level * one(*cut)
    return level


def noise(rng, extent, spread, reach, pieces=(), kind=jnp.bfloat16):
    level = block_levels(rng, extent, pieces, -0.22, 0.18) if pieces else 1.0
    entries = jax.random.normal(rng, extent, jnp.float32) * spread * level
    return jnp.minimum(jnp.maximum(entries, -reach), reach).astype(kind)


def setup_inputs(seed: int = 0) -> dict:
    seeds = jax.random.split(jax.random.key(seed), 12)
    return {
        "tokens": noise(seeds[0], (SEQS, SLOTS, D), 1.0, 6.0, ((0, 16), (1, 8))),
        "lengths": draw_lengths(jax.random.fold_in(seeds[11], 71), 0),
        "cotangent": noise(seeds[2], (SEQS, SLOTS, D), 1.0, 6.0, ((0, 16), (1, 8))),
        "gain_one": jnp.clip(1.0 + 0.18 * jax.random.normal(seeds[3], (D,), jnp.float32), 0.099609375, 1.8984375).astype(jnp.bfloat16),
        "in_weight": noise(seeds[4], (D, 3 * D), D ** -0.5, 0.15625, ((0, 16),)),
        "conv_weight": noise(seeds[5], (3, D), 0.5, 3.0, ((1, 16),)),
        "out_weight": noise(seeds[6], (D, D), D ** -0.5, 0.15625, ((0, 16),)),
        "gain_two": jnp.clip(1.0 + 0.18 * jax.random.normal(seeds[7], (D,), jnp.float32), 0.099609375, 1.8984375).astype(jnp.bfloat16),
        "gate_weight": noise(seeds[8], (D, FF), D ** -0.5, 0.15625, ((0, 16),)),
        "up_weight": noise(seeds[9], (D, FF), D ** -0.5, 0.15625, ((0, 16),)),
        "down_weight": noise(seeds[10], (FF, D), FF ** -0.5, 0.078125, ((0, 16),)),
    }


epsilon = 1e-05
precise_mode = lax.Precision.HIGHEST

@jax.custom_vjp
def low(v):
    return lax.optimization_barrier(v.astype(jnp.bfloat16)).astype(jnp.float32)

@jax.custom_vjp
def low_back(v):
    return v

def low_keep(v):
    return (low(v), None)

def low_pass(kept, grad):
    return (grad,)

def back_keep(v):
    return (v, None)

def back_low(kept, grad):
    return (low(grad),)
low.defvjp(low_keep, low_pass)
low_back.defvjp(back_keep, back_low)

def project(value_rows, weight_matrix):
    return jnp.einsum('pum,my->puy', value_rows, weight_matrix, precision=precise_mode)

def rms_scaled(value_rows, gain):
    return value_rows * lax.rsqrt(lax.optimization_barrier(jnp.mean(value_rows * value_rows, axis=-1, keepdims=True)) + epsilon) * gain

def block(hidden, gain_one, in_weight, conv_weight, out_weight, gain_two, gate_weight, up_weight, down_weight, valid_rows):
    width = hidden.shape[-1]
    normed = low(rms_scaled(hidden, gain_one))
    triple = low_back(project(normed, in_weight))
    input_gate = triple[..., :width]
    output_gate = triple[..., width:2 * width]
    conv_values = triple[..., 2 * width:]
    gated_in = input_gate * conv_values
    extended = jnp.pad(gated_in, ((0, 0), (2, 0), (0, 0)))
    conv_out = conv_weight[0] * extended[:, :-2] + conv_weight[1] * extended[:, 1:-1] + conv_weight[2] * extended[:, 2:]
    mixed = low(output_gate * conv_out)
    middle = hidden + low_back(project(mixed, out_weight))
    normed_two = low(rms_scaled(middle, gain_two))
    gate_pre = low_back(project(normed_two, gate_weight))
    up_pre = low_back(project(normed_two, up_weight))
    active = low(jax.nn.silu(gate_pre) * up_pre)
    return valid_rows[..., None] * (middle + low_back(project(active, down_weight)))

def reference(tokens, lengths, cotangent, gain_one, in_weight, conv_weight, out_weight, gain_two, gate_weight, up_weight, down_weight):
    group_size = max(1, min(SEQS, 4096 // SLOTS))
    while SEQS % group_size:
        group_size = group_size - 1
    groups = SEQS // group_size
    weights = tuple((weight.astype(jnp.float32) for weight in (gain_one, in_weight, conv_weight, out_weight, gain_two, gate_weight, up_weight, down_weight)))
    position = jnp.arange(SLOTS, dtype=jnp.int32)
    valid_all = (position[None, :] < lengths[:, None]).astype(jnp.float32)
    token_groups = tokens.astype(jnp.float32).reshape(groups, group_size, SLOTS, D)
    cot_groups = cotangent.astype(jnp.float32).reshape(groups, group_size, SLOTS, D)
    valid_groups = valid_all.reshape(groups, group_size, SLOTS)

    def advance(carry, member):
        hidden, gradient_output, valid_rows = member

        def forward(hidden_in, *params):
            return block(hidden_in, *params, valid_rows)
        result, pullback = jax.vjp(forward, hidden, *weights)
        grads = pullback(gradient_output)
        summed = tuple((total + part for total, part in zip(carry, grads[1:])))
        return (summed, (result.astype(jnp.bfloat16), grads[0]))
    initial = tuple((jnp.zeros_like(weight) for weight in weights))
    summed, (outputs, grad_hidden) = lax.scan(advance, initial, (token_groups, cot_groups, valid_groups))
    output = outputs.reshape(SEQS, SLOTS, D)
    grad_tokens = grad_hidden.reshape(SEQS, SLOTS, D)
    return (output, grad_tokens, summed[0], summed[1], summed[2], summed[3], summed[4], summed[5], summed[6], summed[7])
```

```python
import jax
import jax.numpy as jnp
from jax import lax
from jax.experimental import pallas as pl
from jax.experimental.pallas import tpu as pltpu
from jax.sharding import Mesh
from jax.sharding import PartitionSpec as P

epsilon = 1e-05
bf16 = jnp.bfloat16
f32 = jnp.float32
ring = ("xh", "xl")
owners = ("y", "xl", "core")
blocks = ("z", "xh")
lane = 128


def shift(value, axis, distance):
    if distance == 0:
        return value
    size = lax.axis_size(axis)
    return lax.ppermute(value, axis, [(i, (i + distance) % size) for i in range(size)])


def matmul(left, right):
    return jnp.dot(left, right, preferred_element_type=f32)


def matmul_right_t(left, right):
    return lax.dot_general(left, right, (((1,), (1,)), ((), ())), preferred_element_type=f32)


def matmul_left_t(left, right):
    return lax.dot_general(left, right, (((0,), (0,)), ((), ())), preferred_element_type=f32)


def gather_z(value):
    return [value] + [shift(value, "z", distance) for distance in (1, 2, 3)]


def scatter_z(parts):
    total = parts[0].astype(f32)
    for distance in (1, 2, 3):
        total = total + shift(parts[distance].astype(bf16), "z", -distance).astype(f32)
    return total


def in_order(parts, axis):
    place = lax.axis_index(axis)
    stacked = jnp.stack(parts)
    return [lax.dynamic_index_in_dim(stacked, (place - i) % 4, axis=0, keepdims=False) for i in range(4)]


def spread_rows(rows, direct=False):
    if direct:
        own = jnp.concatenate(in_order([rows] + [shift(rows, "y", d) for d in (1, 2, 3)], "y"), axis=0)
    else:
        own = lax.all_gather(rows, "y", axis=0, tiled=True)
    half = own.shape[0] // 2
    above = shift(own[:half], ring, 1)
    below = shift(own[half:], ring, -1)
    this_core = jnp.concatenate([own, above, below], axis=0)
    return this_core, shift(this_core, "core", 1)


def combine_rows(left, right, extra=None):
    width = left.shape[1]
    half, quarter = width // 2, width // 4

    def product(start, stop):
        out = matmul_left_t(left[:, start:stop], right)
        if extra is not None:
            out = out + jnp.pad(extra[start:stop], ((0, 0), (right.shape[1] - extra.shape[1], 0)))
        return out

    other_core = product(half, width).astype(bf16)
    arrived = shift(other_core, "core", 1)
    other_x = (product(quarter, half) + arrived[quarter:].astype(f32)).astype(bf16)
    cut = quarter // 2
    above = shift(other_x[:cut], ring, 1)
    below = shift(other_x[cut:], ring, -1)
    mine = product(0, quarter) + arrived[:quarter].astype(f32)
    mine = (mine + jnp.concatenate([above, below], axis=0).astype(f32)).astype(bf16)
    mine = lax.psum_scatter(mine, "y", scatter_dimension=0, tiled=True)
    return add_partner(mine)


def add_partner(mine):
    return (mine.astype(f32) + shift(mine, "xh", 1).astype(f32)).astype(bf16)


def normalize(value_rows, gain):
    scale = lax.rsqrt(jnp.mean(value_rows * value_rows, axis=-1, keepdims=True) + epsilon)
    base = value_rows * scale
    return (base, scale, (base * gain).astype(bf16))


def norm_back(gradient_normalized, base, scale, gain):
    grad_base = gradient_normalized * gain
    return scale * (grad_base - base * jnp.mean(grad_base * base, axis=-1, keepdims=True))


def place_rows(pieces, starts, total):
    rows, width = pieces[0].shape
    gap = total - rows * len(pieces)

    def body(starts_ref, *refs):
        sources, target, sems = refs[: len(pieces)], refs[-2], refs[-1]
        copies = []
        for i, source in enumerate(sources):
            at = pl.ds(pl.multiple_of(starts_ref[i], 16), rows)
            copies.append(pltpu.make_async_copy(source, target.at[at], sems.at[i]))
        for copy in copies:
            copy.start()
        blank = pl.multiple_of(starts_ref[len(pieces)], 16)
        target[pl.ds(blank, gap), :] = jnp.zeros((gap, width), target.dtype)
        for copy in copies:
            copy.wait()

    return pl.pallas_call(
        body,
        out_shape=jax.ShapeDtypeStruct((total, width), pieces[0].dtype),
        in_specs=[pl.BlockSpec(memory_space=pltpu.SMEM)] + [pl.BlockSpec(memory_space=pl.ANY)] * len(pieces),
        out_specs=pl.BlockSpec(memory_space=pltpu.VMEM),
        scratch_shapes=[pltpu.SemaphoreType.DMA((len(pieces),))],
        compiler_params=pltpu.CompilerParams(vmem_limit_bytes=32 * 1024 * 1024),
    )(starts, *pieces)


def local(
    tokens,
    lengths,
    cotangent,
    gain_one,
    in_weight,
    conv_weight,
    out_weight,
    gain_two,
    gate_weight,
    up_weight,
    down_weight,
):
    rows, width = tokens.shape[1:]
    z, xh, xl, core = (lax.axis_index(name) for name in ("z", "xh", "xl", "core"))
    y = lax.axis_index("y")
    own_rows = width // 16
    part = width // 4
    hidden_rows = down_weight.shape[0]
    hidden = 4 * hidden_rows
    padded = -(-hidden // lane) * lane
    gap = padded - hidden
    odd = z % 2

    position = (z * 2 + xh) * rows + jnp.arange(rows, dtype=jnp.int32)
    valid = (position < lengths[0]).astype(f32)[:, None]
    tokens_here = tokens[0]
    value_here = tokens_here.astype(f32)
    grad_result = valid * cotangent[0].astype(f32)
    grad_branch = grad_result.astype(bf16)

    index = jnp.arange(width, dtype=jnp.int32)
    row, piece = index % own_rows, index // own_rows
    source = (((piece % 4) * 2 + ((piece // 4) % 2 ^ xl)) * 2 + (piece // 8 ^ core)) * own_rows + row
    order = (index[:, None] == source[None, :]).astype(bf16)
    channel = (index + z * part) % width
    channel_order = (channel[:, None] == source[None, :]).astype(bf16)

    def to_rows(values):
        return matmul(values, order).astype(bf16)

    def from_rows(values):
        high = values.astype(bf16)
        low = (values - high.astype(f32)).astype(bf16)
        both = matmul_right_t(jnp.concatenate([high, low], axis=0), order)
        return both[:rows] + both[rows:]

    def times(values, halves):
        half = width // 2
        return matmul(values[:, :half], halves[0]) + matmul(values[:, half:], halves[1])

    def times_t(values, halves):
        return jnp.concatenate([matmul_right_t(values, halves[0]), matmul_right_t(values, halves[1])], axis=1)

    in_slice = lax.dynamic_slice_in_dim(in_weight.reshape(own_rows, 3, width), z * part, part, axis=2)
    small = jnp.concatenate([gain_one[:, None], gain_two[:, None], conv_weight.T], axis=1)
    small = jnp.pad(small, ((0, 0), (0, lane - 5)))
    in_slice = jnp.concatenate([in_slice.reshape(own_rows, 3 * part), small], axis=1)
    in_halves = spread_rows(in_slice, direct=True)
    value_all = jnp.concatenate(gather_z(to_rows(tokens_here)), axis=0).astype(f32)
    small = jnp.concatenate([half[:, 3 * part :] for half in in_halves], axis=0)
    gain_rows = small[:, 0].astype(f32)
    small = lax.dot_general(small, order, (((0,), (1,)), ((), ())), preferred_element_type=f32)
    gain_first, gain_second = small[0], small[1]
    taps = lax.dynamic_slice_in_dim(small[2:5], z * part, part, axis=1)
    out_halves = spread_rows(out_weight)
    first_lane = (z * hidden // lane) * lane
    lane_index = jnp.arange(padded, dtype=jnp.int32) - gap * odd
    keep = ((lane_index >= 0) & (lane_index < hidden))[None, :]
    pair_slice = jnp.concatenate(
        [
            jnp.where(keep, lax.dynamic_slice_in_dim(w, first_lane, padded, axis=1), 0).astype(bf16)
            for w in (gate_weight, up_weight)
        ],
        axis=1,
    )
    pair_halves = spread_rows(pair_slice)

    grad_blocks = gather_z(grad_branch)

    down_quarter = lax.dynamic_slice_in_dim(down_weight, ((z - y) % 4) * part, part, axis=1)
    down_quarter = lax.all_gather(down_quarter, "y", axis=0, tiled=False)
    pieces = [
        shift(lax.dynamic_index_in_dim(down_quarter, (z + d) % 4, axis=0, keepdims=False), "z", d) for d in range(4)
    ]
    down_own = jnp.concatenate([pieces[0], pieces[3], pieces[2], pieces[1]], axis=1)
    down_above = shift(down_own[:, : width // 2], ring, 1)
    down_below = shift(down_own[:, width // 2 :], ring, -1)
    down_this = jnp.stack([down_own, jnp.concatenate([down_above, down_below], axis=1)])
    down_other = shift(down_this, "core", 1)
    down_start = [
        gap * odd + hidden_rows * ((xl ^ x) * 2 + (core ^ c)) for c in range(2) for x in range(2)
    ]
    starts = jnp.stack(down_start + [jnp.where(odd == 1, 0, hidden)]).astype(jnp.int32)
    down = place_rows([down_this[0], down_this[1], down_other[0], down_other[1]], starts, padded)

    normed = normalize(value_all, gain_rows)[2]
    base_one, scale_one, _ = normalize(value_here, gain_first)
    triple = times(normed, in_halves).reshape(4, rows, 3 * part + lane)
    input_gate, output_gate, conv_values = (triple[..., i * part : (i + 1) * part] for i in range(3))
    gated_in = input_gate * conv_values
    tails = shift(gated_in[:, rows - 2 :], "xh", 1)
    block_z = (z - jnp.arange(4)) % 4
    first = ((block_z == 0) & (xh == 0))[:, None, None]
    tails = jnp.where(xh == 1, tails, jnp.roll(tails, -1, axis=0))
    tails = jnp.where(first, 0.0, tails)
    extended = jnp.concatenate([tails, gated_in], axis=1)
    conv_out = taps[0] * extended[:, :rows] + taps[1] * extended[:, 1 : rows + 1] + taps[2] * extended[:, 2:]
    mixed = (output_gate * conv_out).astype(bf16)
    mixed = jnp.concatenate([mixed[0]] + [shift(mixed[d], "z", -d) for d in (1, 2, 3)], axis=1)
    mixed = matmul(mixed, channel_order).astype(bf16)
    middle = value_here + times(mixed, out_halves)

    base_two, scale_two, normed_two = normalize(middle, gain_second)
    normed_two = jnp.concatenate(gather_z(to_rows(normed_two)), axis=0)
    grad_all = jnp.concatenate(grad_blocks, axis=0)
    pre = times(normed_two, pair_halves)
    gate_pre, up_pre = pre[:, :padded], pre[:, padded:]
    sigmoid_gate = jax.nn.sigmoid(gate_pre)
    silu_gate = gate_pre * sigmoid_gate
    active = (silu_gate * up_pre).astype(bf16)
    grad_active = matmul_right_t(grad_all, down)
    grad_gate = grad_active * up_pre * sigmoid_gate * (1.0 + gate_pre * (1.0 - sigmoid_gate))
    grad_pair = jnp.concatenate([grad_gate.astype(bf16), (grad_active * silu_gate).astype(bf16)], axis=1)
    grad_normed = times_t(grad_pair, pair_halves).astype(bf16).reshape(4, rows, width)
    grad_normed = from_rows(scatter_z(grad_normed))
    branch = matmul(active, down).astype(bf16).reshape(4, rows, width)
    result = valid * (middle + scatter_z(branch))

    pair_w = combine_rows(normed_two, grad_pair)
    pair_w = lax.all_gather(pair_w, "z", axis=0, tiled=False).astype(f32)

    down_w = matmul_left_t(active, grad_all).astype(bf16)
    down_parts = [lax.dynamic_slice_in_dim(down_w, start, hidden_rows, axis=0) for start in down_start]
    arrived = shift(jnp.stack(down_parts[2:]), "core", 1)
    other_x = (down_parts[1].astype(f32) + arrived[1].astype(f32)).astype(bf16)
    above = shift(other_x[:, : width // 2], ring, 1)
    below = shift(other_x[:, width // 2 :], ring, -1)
    mine = down_parts[0].astype(f32) + arrived[0].astype(f32)
    mine = (mine + jnp.concatenate([above, below], axis=1).astype(f32)).astype(bf16)
    mine = mine.reshape(hidden_rows, 4, part).transpose(1, 0, 2)
    mine = lax.psum_scatter(mine, "y", scatter_dimension=0, tiled=False)
    mine = lax.all_gather(add_partner(mine), "z", axis=0, tiled=False)
    mine = lax.all_to_all(mine, "y", 0, 0, tiled=True)
    grad_down_w = mine.transpose(1, 0, 2).reshape(hidden_rows, width).astype(f32)

    grad_mid_norm = norm_back(grad_normed, base_two, scale_two, gain_second)
    grad_middle = grad_result + grad_mid_norm
    grad_mixer = grad_middle.astype(bf16)

    grad_mixed = times_t(grad_mixer, out_halves).astype(bf16)
    grad_mixed = matmul_right_t(grad_mixed, channel_order).astype(bf16)
    grad_mixed = jnp.stack([shift(grad_mixed[:, d * part : (d + 1) * part], "z", d) for d in range(4)]).astype(f32)
    grad_output_gate = grad_mixed * conv_out
    grad_conv = grad_mixed * output_gate
    heads = shift(grad_conv[:, :2], "xh", 1)
    heads = jnp.where(xh == 0, heads, jnp.roll(heads, 1, axis=0))
    last = ((block_z == 3) & (xh == 1))[:, None, None]
    heads = jnp.where(last, 0.0, heads)
    following = jnp.concatenate([grad_conv, heads], axis=1)
    grad_gated_in = taps[2] * grad_conv + taps[1] * following[:, 1 : rows + 1] + taps[0] * following[:, 2:]
    grad_taps = jnp.stack([jnp.sum(grad_conv * extended[:, k : k + rows], axis=(0, 1)) for k in range(3)])
    grad_triple = jnp.concatenate(
        [
            (grad_gated_in * conv_values).astype(bf16),
            grad_output_gate.astype(bf16),
            (grad_gated_in * input_gate).astype(bf16),
            jnp.zeros((4, rows, lane), bf16),
        ],
        axis=-1,
    ).reshape(4 * rows, 3 * part + lane)
    grad_first = times_t(grad_triple, in_halves).astype(bf16).reshape(4, rows, width)
    grad_first = from_rows(scatter_z(grad_first))
    grad_hidden_norm = norm_back(grad_first, base_one, scale_one, gain_first)
    grad_tokens = grad_middle + grad_hidden_norm

    out_w = combine_rows(mixed, grad_mixer)
    grad_out_w = sum(block.astype(f32) for block in gather_z(out_w))
    tap_rows = lax.dynamic_update_slice(jnp.zeros((lane, width), bf16), grad_taps.astype(bf16), (0, z * part))
    tap_rows = lax.dot_general(order, tap_rows, (((0,), (1,)), ((), ())), preferred_element_type=f32)
    in_w = combine_rows(normed, grad_triple, tap_rows)
    in_w = jnp.stack(in_order(gather_z(in_w), "z")).astype(f32)
    grad_in_w = in_w[..., : 3 * part].reshape(4, own_rows, 3, part).transpose(1, 2, 0, 3).reshape(own_rows, 3 * width)
    grad_conv_w = jnp.sum(in_w[..., 3 * part :], axis=0)[:, :3].T
    grad_gain_one = jnp.sum(grad_in_w * in_weight.astype(f32), axis=1) / gain_one.astype(f32)

    def join(pieces):
        a, b, c, d = (pieces[i] for i in range(4))
        edge = padded - lane
        return jnp.concatenate(
            [
                a[:, :edge], a[:, edge:] + b[:, :lane], b[:, lane:],
                c[:, :edge], c[:, edge:] + d[:, :lane], d[:, lane:],
            ],
            axis=1,
        )

    grad_gate_w = join(pair_w[..., :padded])
    grad_up_w = join(pair_w[..., padded:])

    grad_gain_two = jnp.sum(grad_gate_w * gate_weight.astype(f32) + grad_up_w * up_weight.astype(f32), axis=1)
    grad_gain_two = grad_gain_two / gain_two.astype(f32)

    return (
        result.astype(bf16)[None],
        grad_tokens[None],
        grad_gain_one,
        grad_in_w,
        grad_conv_w,
        grad_out_w,
        grad_gain_two,
        grad_gate_w,
        grad_up_w,
        grad_down_w,
    )


def solution(mesh):
    fine = Mesh(mesh.devices.reshape(4, 2, 4, 2, 2), ("z", "xh", "y", "xl", "core"))
    by_rows = P(owners, None)
    sequences = P(owners, blocks, None)
    return jax.shard_map(
        local,
        mesh=fine,
        in_specs=(
            sequences,
            P(owners),
            sequences,
            P(owners),
            by_rows,
            P(None, owners),
            by_rows,
            P(owners),
            by_rows,
            by_rows,
            by_rows,
        ),
        out_specs=(
            sequences,
            sequences,
            P(owners),
            by_rows,
            P(None, owners),
            by_rows,
            P(owners),
            by_rows,
            by_rows,
            by_rows,
        ),
        check_vma=False,
    )
```

```python
import jax
import jax.numpy as jnp
from jax import lax
from jax.experimental import pallas as pl
from jax.experimental.pallas import tpu as pltpu
from jax.sharding import Mesh
from jax.sharding import PartitionSpec as P

epsilon = 1e-05
bf16 = jnp.bfloat16
f32 = jnp.float32
ring = ("xh", "xl")
owners = ("y", "xl", "core")
blocks = ("z", "xh")
lane = 128
MiB = 1024 * 1024
scope = jax.named_scope
wide = 112


def shift(value, axis, distance):
    if distance == 0:
        return value
    size = lax.axis_size(axis)
    return lax.ppermute(value, axis, [(i, (i + distance) % size) for i in range(size)])


def matmul(left, right):
    return jnp.dot(left, right, preferred_element_type=f32)


def matmul_right_t(left, right):
    return lax.dot_general(left, right, (((1,), (1,)), ((), ())), preferred_element_type=f32)


def exchange(value, axis):
    return lax.all_to_all(value, axis, 0, 0, tiled=True)


def gather_now(value, axis):
    return exchange(jnp.broadcast_to(value[None], (4,) + value.shape), axis)


def in_order(parts, axis):
    place = lax.axis_index(axis)
    stacked = jnp.stack(parts)
    return [lax.dynamic_index_in_dim(stacked, (place - i) % 4, axis=0, keepdims=False) for i in range(4)]


def along(value, axis):
    return [value] + [shift(value, axis, d) for d in (1, 2, 3)]


def across_x(upper, lower):
    return shift(upper, ring, 1), shift(lower, ring, -1)


def by_half(rows):
    half = rows.shape[0] // 2
    return rows[:half], rows[half:]


def add_partner(mine):
    return (mine.astype(f32) + shift(mine, "xh", 1).astype(f32)).astype(bf16)


def sum_y(mine):
    return jnp.sum(exchange(mine, "y").astype(f32), axis=0).astype(bf16)


def corner(value):
    return value[(0,) * (value.ndim - 2)][:16, :lane]


def tie(value, *others):
    others = [corner(other) for other in others]
    return pl.pallas_call(
        lambda *refs: None,
        out_shape=jax.ShapeDtypeStruct(value.shape, value.dtype),
        in_specs=[pl.BlockSpec(memory_space=pltpu.HBM)] * (1 + len(others)),
        out_specs=pl.BlockSpec(memory_space=pltpu.HBM),
        input_output_aliases={0: 0},
        compiler_params=pltpu.CompilerParams(vmem_limit_bytes=128 * 1024),
        cost_estimate=pl.CostEstimate(flops=0, bytes_accessed=0, transcendentals=0),
    )(value, *others)


def whole(shape):
    return pl.BlockSpec(shape, lambda *at: (0,) * len(shape))


def columns(rows, chunk, first=0):
    return pl.BlockSpec((rows, chunk), lambda j: (0, first + j))


def scaled(values):
    scale = lax.rsqrt(jnp.mean(values * values, axis=-1, keepdims=True) + epsilon)
    return values * scale, scale


def norm_back(gradient_normalized, base, scale, gain):
    grad_base = gradient_normalized * gain
    return scale * (grad_base - base * jnp.mean(grad_base * base, axis=-1, keepdims=True))


def vmem():
    return pltpu.CompilerParams(vmem_limit_bytes=56 * MiB)


def smem():
    return pl.BlockSpec(memory_space=pltpu.SMEM)


def lay(parts, places_ref, target):
    rows = target.shape[0] // 16
    i = 0
    for part in parts:
        for k in range(part.shape[0]):
            target[pl.ds(pl.multiple_of(places_ref[i] * rows, 16), rows), :] = part[k]
            i += 1


def in_projection(values, pieces, places):
    tokens, width = values.shape
    rows = tokens // 4
    outer = pieces[0].shape[2]
    inner = outer - lane

    def body(places_ref, v_ref, *refs):
        parts, (normed_ref, out_ref, small_ref, w_ref) = refs[:-4], refs[-4:]

        @pl.when(pl.program_id(0) == 0)
        def _():
            lay(parts, places_ref, w_ref)
            small_ref[...] = w_ref[:, inner:].astype(f32).T[:8, :]

        base, _ = scaled(v_ref[...].astype(f32))
        normed_ref[...] = (base * small_ref[:1, :]).astype(bf16)
        out_ref[...] = matmul(normed_ref[...], w_ref[:, :inner])

    by_rows = pl.BlockSpec((rows, width), lambda j: (j, 0))
    return pl.pallas_call(
        body,
        grid=(4,),
        in_specs=[smem(), by_rows] + [whole(p.shape) for p in pieces],
        out_specs=[by_rows, pl.BlockSpec((rows, inner), lambda j: (j, 0)), whole((8, width)), whole((width, outer))],
        out_shape=[
            jax.ShapeDtypeStruct((tokens, width), bf16),
            jax.ShapeDtypeStruct((tokens, inner), f32),
            jax.ShapeDtypeStruct((8, width), f32),
            jax.ShapeDtypeStruct((width, outer), bf16),
        ],
        compiler_params=vmem(),
    )(places, values, *pieces)


def out_projection(place, values, mixed, weight, gain):
    rows, width = values.shape
    part = width // 4

    def body(z_ref, v_ref, *refs):
        blocks, (w_ref, gain_ref, mixed_ref, middle_ref, normed_ref) = refs[:4], refs[4:]
        for d in range(4):
            at = pl.multiple_of(lax.rem(z_ref[0] + d, 4) * part, lane)
            mixed_ref[:, pl.ds(at, part)] = blocks[d][...]
        middle = v_ref[...].astype(f32) + matmul(mixed_ref[...], w_ref[...])
        middle_ref[...] = middle
        base, _ = scaled(middle)
        normed_ref[...] = (base * gain_ref[...]).astype(bf16)

    return pl.pallas_call(
        body,
        in_specs=[smem(), whole(values.shape)] + [whole((rows, part))] * 4 + [whole(weight.shape), whole(gain.shape)],
        out_specs=[whole((rows, width))] * 3,
        out_shape=[jax.ShapeDtypeStruct((rows, width), t) for t in (bf16, f32, bf16)],
        grid=(1,),
        compiler_params=vmem(),
    )(place, values, *mixed, weight, gain)


def summed(parts):
    total = parts[0][...].astype(f32)
    for part in parts[1:]:
        total = total + part[...].astype(f32)
    return total


def middle_back(place, parts, middle, gain, grad_result, weight):
    rows, width = middle.shape
    part = width // 4

    def body(z_ref, middle_ref, gain_ref, result_ref, w_ref, *refs):
        parts, (grad_ref, mixer_ref, *mixed_refs) = refs[:4], refs[4:]
        base, scale = scaled(middle_ref[...])
        grad = result_ref[...] + norm_back(summed(parts), base, scale, gain_ref[...])
        grad_ref[...] = grad
        mixer_ref[...] = grad.astype(bf16)
        for d in range(4):
            at = pl.ds(pl.multiple_of(lax.rem(z_ref[0] + d, 4) * part, lane), part)
            mixed_refs[d][...] = matmul_right_t(mixer_ref[...], w_ref[at, :]).astype(bf16)

    return pl.pallas_call(
        body,
        in_specs=[smem()] + [whole(a.shape) for a in (middle, gain, grad_result, weight, *parts)],
        out_specs=[whole((rows, width))] * 2 + [whole((rows, part))] * 4,
        out_shape=[jax.ShapeDtypeStruct((rows, width), t) for t in (f32, bf16)]
        + [jax.ShapeDtypeStruct((rows, part), bf16)] * 4,
        grid=(1,),
        compiler_params=vmem(),
    )(place, middle, gain, grad_result, weight, *parts)


def token_back(parts, tokens, gain, grad_middle):
    rows, width = tokens.shape

    def body(tokens_ref, gain_ref, middle_ref, *refs):
        base, scale = scaled(tokens_ref[...].astype(f32))
        refs[4][...] = middle_ref[...] + norm_back(summed(refs[:4]), base, scale, gain_ref[...])

    return pl.pallas_call(
        body,
        in_specs=[whole(a.shape) for a in (tokens, gain, grad_middle, *parts)],
        out_specs=whole((rows, width)),
        out_shape=jax.ShapeDtypeStruct((rows, width), f32),
        grid=(1,),
        compiler_params=vmem(),
    )(tokens, gain, grad_middle, *parts)


def in_projection_back(grad_mixed, heads, conv_out, triple, taps, weight):
    blocks, rows, part = grad_mixed.shape
    inner = 3 * part
    width = weight.shape[0]

    def body(grad_ref, heads_ref, conv_ref, triple_ref, taps_ref, w_ref, out_ref, parts_ref):
        grad_mixed = grad_ref[0].astype(f32)
        grad_conv = grad_mixed * triple_ref[:, part : 2 * part]
        row = lax.broadcasted_iota(jnp.int32, (rows, part), 0)
        first, second = heads_ref[0, 0:1, :], heads_ref[0, 1:2, :]
        one = jnp.where(row == rows - 1, first, pltpu.roll(grad_conv, rows - 1, 0))
        two = pltpu.roll(grad_conv, rows - 2, 0)
        two = jnp.where(row == rows - 2, first, jnp.where(row == rows - 1, second, two))
        grad = taps_ref[2:3, :] * grad_conv + taps_ref[1:2, :] * one + taps_ref[0:1, :] * two
        out_ref[:, :part] = (grad * triple_ref[:, 2 * part : inner]).astype(bf16)
        out_ref[:, part : 2 * part] = (grad_mixed * conv_ref[0]).astype(bf16)
        out_ref[:, 2 * part : inner] = (grad * triple_ref[:, :part]).astype(bf16)
        out_ref[:, inner:] = jnp.zeros((rows, lane), bf16)
        parts_ref[0] = matmul_right_t(out_ref[:, :inner], w_ref[:, :inner]).astype(bf16)

    def block(*shape):
        return pl.BlockSpec((1, *shape), lambda j: (j, 0, 0))

    return pl.pallas_call(
        body,
        grid=(blocks,),
        in_specs=[
            block(rows, part),
            block(2, part),
            block(rows, part),
            pl.BlockSpec((rows, inner), lambda j: (j, 0)),
            whole(taps.shape),
            whole(weight.shape),
        ],
        out_specs=[pl.BlockSpec((rows, inner + lane), lambda j: (j, 0)), block(rows, width)],
        out_shape=[
            jax.ShapeDtypeStruct((blocks * rows, inner + lane), bf16),
            jax.ShapeDtypeStruct((blocks, rows, width), bf16),
        ],
        compiler_params=vmem(),
    )(grad_mixed, heads, conv_out, triple, taps, weight)


def turn(left, places, turned, moved):
    turned[...] = left[...].T
    rows = turned.shape[0] // 16
    for i in range(16):
        at = pl.multiple_of(places[i] * rows, 16)
        moved[i * rows : (i + 1) * rows, :] = turned[pl.ds(at, rows), :]


def mixer_gradients(normed, grad_triple, places, extra, grad_mixer, mixed):
    tokens, width = normed.shape
    inner, part = grad_triple.shape[1], mixed.shape[1]
    half = width // 2

    def body(places_ref, normed_ref, triple_ref, extra_ref, mixer_ref, mixed_ref, send_ref, keep_ref, turned, moved):
        for left, right, at in (
            (normed_ref, triple_ref, slice(0, inner)),
            (mixer_ref, mixed_ref, slice(inner, inner + part)),
        ):
            turn(left, places_ref, turned, moved)
            for ref, start in ((keep_ref, 0), (send_ref, half)):
                ref[:, at] = matmul(moved[start : start + half, :], right[...]).astype(bf16)
        rows = width // 16
        for i in range(16):
            ref = keep_ref if i < 8 else send_ref
            at = pl.multiple_of(places_ref[i] * rows, 16)
            ref[i % 8 * rows : (i % 8 + 1) * rows, inner - lane : inner] = extra_ref[pl.ds(at, rows), :]

    return pl.pallas_call(
        body,
        grid=(1,),
        in_specs=[smem()] + [whole(a.shape) for a in (normed, grad_triple, extra, grad_mixer, mixed)],
        out_specs=[whole((half, inner + part))] * 2,
        out_shape=[jax.ShapeDtypeStruct((half, inner + part), bf16)] * 2,
        scratch_shapes=[pltpu.VMEM((width, tokens), bf16)] * 2,
        compiler_params=vmem(),
    )(places, normed, grad_triple, extra, grad_mixer, mixed)


def feed_forward(normed, grads, weights, places, down):
    tokens, width = normed.shape
    padded = down.shape[0]
    chunk = 256
    steps = padded // chunk
    pieces = len(weights)
    rows = tokens // 4

    def body(places_ref, n_ref, g_ref, *refs):
        gates, ups = refs[:pieces], refs[pieces : 2 * pieces]
        d_ref, active_ref, pair_ref, *out_refs, gate_w, up_w, all_w, all_grads = refs[2 * pieces :]
        step = pl.program_id(0)
        lay(gates, places_ref, gate_w)
        lay(ups, places_ref, up_w)
        here = pl.ds(pl.multiple_of(step * chunk, chunk), chunk)
        later = pl.ds(pl.multiple_of(padded + step * chunk, chunk), chunk)
        all_w[:, here] = gate_w[...]
        all_w[:, later] = up_w[...]
        gate = matmul(n_ref[...], gate_w[...])
        up = matmul(n_ref[...], up_w[...])
        grad = matmul_right_t(g_ref[...], d_ref[...])
        sig = jax.nn.sigmoid(gate)
        silu = gate * sig
        active_ref[...] = (silu * up).astype(bf16)
        gg = (grad * up * sig * (1.0 + gate * (1.0 - sig))).astype(bf16)
        gu = (grad * silu).astype(bf16)
        pair_ref[0] = gg
        pair_ref[1] = gu
        all_grads[:, here] = gg
        all_grads[:, later] = gu

        @pl.when(step == steps - 1)
        def _():
            for at in range(0, width, width // 4):
                at = slice(at, at + width // 4)
                total = matmul_right_t(all_grads[...], all_w[at, :]).astype(bf16)
                for d, out_ref in enumerate(out_refs):
                    out_ref[:, at] = total[d * rows : (d + 1) * rows, :]

    def block(part, first):
        return pl.BlockSpec((*part.shape[:2], chunk), lambda j: (0, 0, first + j))

    return pl.pallas_call(
        body,
        grid=(steps,),
        in_specs=[smem(), whole((tokens, width)), whole((tokens, width))]
        + [block(part, 0) for part in weights]
        + [block(part, steps) for part in weights]
        + [pl.BlockSpec((chunk, width), lambda j: (j, 0))],
        out_specs=[
            columns(tokens, chunk),
            pl.BlockSpec((2, tokens, chunk), lambda j: (0, 0, j)),
        ]
        + [whole((rows, width))] * 4,
        out_shape=[
            jax.ShapeDtypeStruct((tokens, padded), bf16),
            jax.ShapeDtypeStruct((2, tokens, padded), bf16),
        ]
        + [jax.ShapeDtypeStruct((rows, width), bf16)] * 4,
        scratch_shapes=[pltpu.VMEM((width, chunk), bf16)] * 2
        + [pltpu.VMEM((width, 2 * padded), bf16), pltpu.VMEM((tokens, 2 * padded), bf16)],
        compiler_params=vmem(),
    )(places, normed, grads, *weights, *weights, down)


def feed_forward_weights(normed, grads, active, pair, places, place, down):
    tokens, width = normed.shape
    padded = down.shape[0]
    half = width // 2
    rows = tokens // 4
    chunk = 256
    steps = padded // chunk

    def body(places_ref, z_ref, n_ref, g_ref, a_ref, pair_ref, d_ref, *refs):
        send_ref, keep_ref, down_send_ref, down_keep_ref, out_ref, done_ref, turned, moved, down_w, total = refs
        step = pl.program_id(0)

        @pl.when(step == 0)
        def _():
            turn(n_ref, places_ref, turned, moved)
            total[...] = jnp.zeros_like(total)

        for i in range(2):
            keep_ref[i] = matmul(moved[:half, :], pair_ref[i]).astype(bf16)
            send_ref[i] = matmul(moved[half:, :], pair_ref[i]).astype(bf16)
        a = a_ref[...]
        here = pl.ds(pl.multiple_of(step * chunk, chunk), chunk)
        down_w[here, :] = lax.dot_general(a, g_ref[...], (((0,), (0,)), ((), ())), preferred_element_type=f32).astype(bf16)
        total[...] += matmul(a, d_ref[...])

        @pl.when(step == steps - 1)
        def _():
            done_ref[...] = jnp.zeros_like(done_ref)
            for d in range(4):
                out_ref[pl.ds(lax.rem(z_ref[0] + 4 - d, 4), 1)] = total[d * rows : (d + 1) * rows, :].astype(bf16)[None]
            for i in range(16):
                ref = down_keep_ref if i < 8 else down_send_ref
                at = pl.multiple_of(places_ref[i] * wide, 16)
                ref[i % 8 * wide : (i % 8 + 1) * wide, :] = down_w[pl.ds(at, wide), :]

    def both(rows):
        return pl.BlockSpec((2, rows, chunk), lambda j: (0, 0, j))

    return pl.pallas_call(
        body,
        grid=(steps,),
        in_specs=[
            smem(),
            smem(),
            whole((tokens, width)),
            whole((tokens, width)),
            columns(tokens, chunk),
            both(tokens),
            pl.BlockSpec((chunk, width), lambda j: (j, 0)),
        ],
        out_specs=[both(half)] * 2
        + [whole((padded // 2, width))] * 2
        + [whole((4, rows, width)), whole((8, lane))],
        out_shape=[jax.ShapeDtypeStruct((2, half, padded), bf16)] * 2
        + [jax.ShapeDtypeStruct((padded // 2, width), bf16)] * 2
        + [jax.ShapeDtypeStruct((4, rows, width), bf16), jax.ShapeDtypeStruct((8, lane), f32)],
        scratch_shapes=[pltpu.VMEM((width, tokens), bf16)] * 2
        + [pltpu.VMEM((padded, width), bf16), pltpu.VMEM((tokens, width), f32)],
        compiler_params=vmem(),
    )(places, place, normed, grads, active, pair, down)


def pick_hidden(place, gate, up):
    rows, hidden = gate.shape
    owned = hidden // 16
    share = owned // 4
    padded = 16 * wide

    def body(z_ref, gate_ref, up_ref, out_ref):
        for z in range(4):

            @pl.when(z_ref[0] == z)
            def _():
                for i, ref in enumerate((gate_ref, up_ref)):
                    parts = []
                    for d in range(16):
                        start = owned * d + share * z
                        parts += [ref[:, start : start + share], jnp.zeros((rows, wide - share), bf16)]
                    out_ref[:, padded * i : padded * (i + 1)] = jnp.concatenate(parts, axis=1)

    return pl.pallas_call(
        body,
        in_specs=[smem(), whole(gate.shape), whole(up.shape)],
        out_specs=whole((rows, 2 * padded)),
        out_shape=jax.ShapeDtypeStruct((rows, 2 * padded), bf16),
        grid=(1,),
        compiler_params=vmem(),
    )(place, gate, up)


def spread_hidden(parts, gate, up):
    rows, hidden = gate.shape
    owned = hidden // 16
    share = owned // 4
    padded = 16 * wide
    chunk = 16

    def body(parts_ref, gate_ref, up_ref, grad_gate_ref, grad_up_ref, sums_ref):
        sums = None
        for i, (w_ref, out_ref) in enumerate(((gate_ref, grad_gate_ref), (up_ref, grad_up_ref))):
            blocks = [parts_ref[z, i].astype(f32) for z in range(4)]
            pieces = [blocks[z][:, wide * d : wide * d + share] for d in range(16) for z in range(4)]
            out = jnp.concatenate(pieces, axis=1)
            out_ref[...] = out
            term = jnp.sum(out * w_ref[...].astype(f32), axis=1, keepdims=True)
            sums = term if sums is None else sums + term
        sums_ref[...] = jnp.broadcast_to(sums, (chunk, lane))

    by_rows = pl.BlockSpec((chunk, hidden), lambda j: (j, 0))
    return pl.pallas_call(
        body,
        grid=(rows // chunk,),
        in_specs=[pl.BlockSpec((4, 2, chunk, padded), lambda j: (0, 0, j, 0)), by_rows, by_rows],
        out_specs=[by_rows, by_rows, pl.BlockSpec((chunk, lane), lambda j: (j, 0))],
        out_shape=[jax.ShapeDtypeStruct((rows, hidden), f32)] * 2 + [jax.ShapeDtypeStruct((rows, lane), f32)],
        compiler_params=vmem(),
    )(parts, gate, up)


def local(
    tokens,
    lengths,
    cotangent,
    gain_one,
    in_weight,
    conv_weight,
    out_weight,
    gain_two,
    gate_weight,
    up_weight,
    down_weight,
):
    rows, width = tokens.shape[1:]
    z, xh, y, xl, core = (lax.axis_index(name) for name in ("z", "xh", "y", "xl", "core"))
    own_rows = width // 16
    part = width // 4
    quarter = width // 4
    hidden_rows = down_weight.shape[0]
    share = hidden_rows // 4
    padded = 16 * wide

    position = (z * 2 + xh) * rows + jnp.arange(rows, dtype=jnp.int32)
    valid = (position < lengths[0]).astype(f32)[:, None]
    tokens_here = tokens[0]
    grad_result = valid * cotangent[0].astype(f32)
    grad_branch = grad_result.astype(bf16)

    index = jnp.arange(16, dtype=jnp.int32)
    places = ((index % 4) * 2 + (index // 4 % 2 ^ xl)) * 2 + (index // 8 ^ core)
    places_behind = (((y - index) % 4) * 2 + (index // 4 % 2 ^ xl)) * 2 + (index // 8 ^ core)

    def gather(value):
        return lax.all_gather(value, owners, axis=0, tiled=True)

    def both_cores(parts):
        return parts + [shift(part, "core", 1) for part in parts]

    def send_back(parts):
        return [shift(parts[d], "z", -d) for d in range(4)]

    with scope("in_y"):
        small = jnp.concatenate([gain_one[:, None], gain_two[:, None], conv_weight.T], axis=1)
        in_slice = [lax.dynamic_slice_in_dim(in_weight, i * width + z * part, part, axis=1) for i in range(3)]
        in_y = gather_now(jnp.concatenate(in_slice + [jnp.pad(small, ((0, 0), (0, lane - 5)))], axis=1), "y")
    with scope("tokens_z"):
        token_parts = along(jnp.stack([tokens_here, grad_branch]), "z")
    with scope("out_all"):
        out_all = gather(out_weight)
    with scope("in_x"):
        in_pieces = both_cores([in_y, *across_x(*by_half(in_y))])
    with scope("pair_y"):
        pair_slice = pick_hidden(z[None], gate_weight, up_weight)
        pair_y = gather_now(tie(pair_slice, in_y), "y")
    with scope("down_all"):
        down_slice = lax.dynamic_slice_in_dim(down_weight, z * share, share, axis=0)
        down_all = gather(jnp.pad(down_slice, ((0, wide - share), (0, 0))))

    with scope("triple"):
        value_all = jnp.concatenate([block[0] for block in token_parts], axis=0)
        grad_all = jnp.concatenate([block[1] for block in token_parts], axis=0)
        normed, triple, small, in_all = in_projection(value_all, in_pieces, places)
        gain_first, gain_second = small[0:1], small[1:2]
        taps = lax.dynamic_slice_in_dim(small[2:5], z * part, part, axis=1)
        triple_blocks = triple.reshape(4, rows, 3 * part)
        output_gate = triple_blocks[..., part : 2 * part]
        gated_in = triple_blocks[..., :part] * triple_blocks[..., 2 * part :]
        tails = shift(gated_in[:, rows - 2 :], "xh", 1)
    with scope("conv"):
        block_z = (z - jnp.arange(4)) % 4
        first = ((block_z == 0) & (xh == 0))[:, None, None]
        tails = jnp.where(xh == 1, tails, jnp.roll(tails, -1, axis=0))
        tails = jnp.where(first, 0.0, tails)
        extended = jnp.concatenate([tails, gated_in], axis=1)
        conv_out = taps[0] * extended[:, :rows] + taps[1] * extended[:, 1 : rows + 1] + taps[2] * extended[:, 2:]
        mixed = (output_gate * conv_out).astype(bf16)
        pair_y = tie(pair_y, mixed)
        mixed_blocks = mixed
        mixed = send_back(mixed)
    with scope("pair_x"):
        pair_x = across_x(*by_half(pair_y))
        pair_y_other = shift(pair_y, "core", 1)
    with scope("out_projection"):
        mixed = [tie(mixed[0], pair_y_other), *mixed[1:]]
        mixed, middle, normed_two = out_projection(z[None], tokens_here, mixed, out_all, gain_second)
    with scope("normed_z"):
        normed_all = gather_now(normed_two, "z")
        normed_all = [lax.dynamic_index_in_dim(normed_all, (z - d) % 4, axis=0, keepdims=False) for d in range(4)]
        normed_all = jnp.concatenate(normed_all, axis=0)
    with scope("pair_core"):
        pair_x = [tie(part, normed_all) for part in pair_x]
        pair_pieces = [pair_y, *pair_x, pair_y_other, *(shift(part, "core", 1) for part in pair_x)]

    with scope("feed_forward"):
        active, grad_pair, *grad_parts = feed_forward(normed_all, grad_all, pair_pieces, places, down_all)
        grad_parts = send_back(grad_parts)
    with scope("feed_forward_weights"):
        pair_send, pair_keep, down_send, down_keep, branch, done = feed_forward_weights(
            normed_all, grad_all, active, grad_pair, places, z[None], down_all
        )
    with scope("middle_back"):
        grad_middle, grad_mixer, *grad_mixed = middle_back(
            z[None], [tie(grad_parts[0], done), *grad_parts[1:]], middle, gain_second, grad_result, out_all
        )
        grad_mixed = jnp.stack([shift(grad_mixed[d], "z", d) for d in range(4)])
    with scope("pair_wcore"):
        pair_core = shift(tie(pair_send, grad_mixer), "core", 1)
    with scope("down_wcore"):
        down_core = shift(tie(down_send, grad_mixer), "core", 1)
    with scope("heads"):
        heads = shift(grad_mixed[:, :2].astype(f32) * output_gate[:, :2], "xh", 1)
    with scope("pair_wx"):
        pair_core = tie(pair_core, heads)
        pair_x = (pair_keep[:, quarter:].astype(f32) + pair_core[:, quarter:].astype(f32)).astype(bf16)
        pair_gate, pair_up = pair_x[0], pair_x[1]
        heads = tie(heads, pair_gate)
        pair_x = across_x(pair_gate, pair_up)
    with scope("branch"):
        branch = lax.psum_scatter(tie(branch, heads), "z", scatter_dimension=0, tiled=False)
    with scope("down_wx"):
        eighth = padded // 4
        down_core = tie(down_core, pair_gate)
        down_x = (down_keep[eighth:].astype(f32) + down_core[eighth:].astype(f32)).astype(bf16)
        down_upper, down_lower = by_half(down_x)
        heads = tie(heads, down_upper)
        down_x = across_x(down_upper, down_lower)
    with scope("triple_back"):
        heads = jnp.where(xh == 0, heads, jnp.roll(heads, 1, axis=0))
        last = ((block_z == 3) & (xh == 1))[:, None, None]
        heads = jnp.where(last, 0.0, heads)
        grad_triple, grad_parts = in_projection_back(grad_mixed, heads, conv_out, triple, taps, in_all)
        grad_first = send_back(grad_parts)
    with scope("out_z"):
        mixer_all = gather_now(tie(grad_mixer, grad_parts), "z")
    with scope("taps_back"):
        grad_conv = grad_mixed.astype(f32) * output_gate
        grad_taps = jnp.stack([jnp.sum(grad_conv * extended[:, k : k + rows], axis=(0, 1)) for k in range(3)])
        grad_taps = jnp.pad(grad_taps, ((0, lane - 3), (0, 0))).T.astype(bf16)
        grad_taps = lax.dynamic_update_slice(jnp.zeros((width, lane), bf16), grad_taps, (z * part, 0))
    with scope("pair_wy"):
        mine = pair_keep[:, :quarter].astype(f32) + pair_core[:, :quarter].astype(f32)
        mine = (mine + jnp.stack([tie(pair_x[0], grad_parts, branch), pair_x[1]]).astype(f32)).astype(bf16)
        pair_mine = mine.reshape(2, 4, own_rows, padded).transpose(1, 0, 2, 3)
        pair_w = exchange(pair_mine, "y")
    with scope("in_w"):
        mixer_all = [lax.dynamic_index_in_dim(mixer_all, (z - d) % 4, axis=0, keepdims=False) for d in range(4)]
        in_send, in_keep = mixer_gradients(
            tie(normed, pair_mine),
            grad_triple,
            places_behind,
            grad_taps,
            jnp.concatenate(mixer_all, axis=0),
            mixed_blocks.reshape(4 * rows, part),
        )
        in_core = shift(in_send, "core", 1)
    with scope("token_back"):
        grad_tokens = token_back([tie(grad_first[0], in_send), *grad_first[1:]], tokens_here, gain_first, grad_middle)
    with scope("in_wx"):
        in_x = (in_keep[quarter:].astype(f32) + in_core[quarter:].astype(f32)).astype(bf16)
        in_upper, in_lower = by_half(in_x)
        in_x = across_x(in_upper, in_lower)
    with scope("in_wy"):
        mine = in_keep[:quarter].astype(f32) + in_core[:quarter].astype(f32)
        mine = mine + jnp.concatenate([tie(in_x[0], grad_tokens), in_x[1]], axis=0).astype(f32)
        in_mine = mine.astype(bf16).reshape(4, own_rows, -1)
    with scope("pair_wxh"):
        pair_w = jnp.sum(tie(pair_w, grad_tokens, in_mine).astype(f32), axis=0).astype(bf16)
        pair_partner = add_partner(pair_w)
    with scope("in_wy"):
        in_blocks = tie(in_mine, pair_w)
        in_w = in_blocks[0].astype(f32)
        for d in (1, 2, 3):
            in_w = in_w + shift(in_blocks[d], "y", -d).astype(f32)
        in_w = in_w.astype(bf16)
        in_partner = add_partner(in_w)
    with scope("down_wy"):
        down_mine = down_keep[:eighth].astype(f32) + down_core[:eighth].astype(f32)
        down_mine = down_mine + jnp.concatenate([tie(down_x[0], pair_w), down_x[1]], axis=0).astype(f32)
        down_mine = down_mine.astype(bf16).reshape(4, wide, width)
        down_w = lax.psum_scatter(down_mine, "y", scatter_dimension=0, tiled=False)
    with scope("pair_wz"):
        pair_z = gather_now(pair_partner, "z")
    with scope("down_wz"):
        down_w = in_order(along(add_partner(tie(down_w, pair_partner)), "z"), "z")
        grad_down_w = jnp.concatenate([piece[:share] for piece in down_w], axis=0).astype(f32)
    with scope("in_wz"):
        in_w = gather_now(tie(in_partner, pair_z, grad_down_w), "z")
    with scope("out_end"):
        out_w = jnp.concatenate([in_w[d, :, 3 * part + lane :] for d in range(4)], axis=1).T
        out_w = lax.all_to_all(out_w.reshape(16, own_rows, own_rows), owners, 0, 0, tiled=True)
        grad_out_w = out_w.transpose(1, 0, 2).reshape(own_rows, width).astype(f32)
    with scope("result"):
        result = valid * (middle + branch.astype(f32))
    with scope("in_end"):
        in_w = in_w[..., : 3 * part + lane].astype(f32)
        grad_in_w = jnp.concatenate([in_w[d, :, i * part : (i + 1) * part] for i in range(3) for d in range(4)], axis=1)
        grad_conv_w = jnp.sum(in_w[..., 3 * part :], axis=0)[:, :3].T
        grad_gain_one = jnp.sum(grad_in_w * in_weight.astype(f32), axis=1) / gain_one.astype(f32)
    with scope("pair_end"):
        grad_gate_w, grad_up_w, sums = spread_hidden(pair_z, gate_weight, up_weight)
        grad_gain_two = sums[:, 0] / gain_two.astype(f32)

    return (
        result.astype(bf16)[None],
        grad_tokens[None],
        grad_gain_one,
        grad_in_w,
        grad_conv_w,
        grad_out_w,
        grad_gain_two,
        grad_gate_w,
        grad_up_w,
        grad_down_w,
    )


def solution(mesh):
    fine = Mesh(mesh.devices.reshape(4, 2, 4, 2, 2), ("z", "xh", "y", "xl", "core"))
    by_rows = P(owners, None)
    sequences = P(owners, blocks, None)
    return jax.shard_map(
        local,
        mesh=fine,
        in_specs=(
            sequences,
            P(owners),
            sequences,
            P(owners),
            by_rows,
            P(None, owners),
            by_rows,
            P(owners),
            by_rows,
            by_rows,
            by_rows,
        ),
        out_specs=(
            sequences,
            sequences,
            P(owners),
            by_rows,
            P(None, owners),
            by_rows,
            P(owners),
            by_rows,
            by_rows,
            by_rows,
        ),
        check_vma=False,
    )
```

```python
import jax
import jax.numpy as jnp
from jax import lax
from jax.experimental import pallas as pl
from jax.experimental.pallas import tpu as pltpu
from jax.sharding import Mesh
from jax.sharding import PartitionSpec as P

epsilon = 1e-05
bf16 = jnp.bfloat16
f32 = jnp.float32
ring = ("xh", "xl")
owners = ("y", "xl", "core")
blocks = ("z", "xh")
lane = 128
MiB = 1024 * 1024
scope = jax.named_scope
wide = 112


def shift(value, axis, distance):
    if distance == 0:
        return value
    size = lax.axis_size(axis)
    return lax.ppermute(value, axis, [(i, (i + distance) % size) for i in range(size)])


def matmul(left, right):
    return jnp.dot(left, right, preferred_element_type=f32)


def matmul_right_t(left, right):
    return lax.dot_general(left, right, (((1,), (1,)), ((), ())), preferred_element_type=f32)


def exchange(value, axis):
    return lax.all_to_all(value, axis, 0, 0, tiled=True)


def gather_now(value, axis):
    return exchange(jnp.broadcast_to(value[None], (4,) + value.shape), axis)


def in_order(parts, axis):
    place = lax.axis_index(axis)
    stacked = jnp.stack(parts)
    return [lax.dynamic_index_in_dim(stacked, (place - i) % 4, axis=0, keepdims=False) for i in range(4)]


def along(value, axis):
    return [value] + [shift(value, axis, d) for d in (1, 2, 3)]


def across_x(upper, lower):
    return shift(upper, ring, 1), shift(lower, ring, -1)


def by_half(rows):
    half = rows.shape[0] // 2
    return rows[:half], rows[half:]


def add_partner(mine):
    return (mine.astype(f32) + shift(mine, "xh", 1).astype(f32)).astype(bf16)


def sum_y(mine):
    return jnp.sum(exchange(mine, "y").astype(f32), axis=0).astype(bf16)


def corner(value):
    return value[(0,) * (value.ndim - 2)][:16, :lane]


def tie(value, *others):
    others = [corner(other) for other in others]
    return pl.pallas_call(
        lambda *refs: None,
        out_shape=jax.ShapeDtypeStruct(value.shape, value.dtype),
        in_specs=[pl.BlockSpec(memory_space=pltpu.HBM)] * (1 + len(others)),
        out_specs=pl.BlockSpec(memory_space=pltpu.HBM),
        input_output_aliases={0: 0},
        compiler_params=pltpu.CompilerParams(vmem_limit_bytes=128 * 1024),
        cost_estimate=pl.CostEstimate(flops=0, bytes_accessed=0, transcendentals=0),
    )(value, *others)


def whole(shape):
    return pl.BlockSpec(shape, lambda *at: (0,) * len(shape))


def columns(rows, chunk, first=0):
    return pl.BlockSpec((rows, chunk), lambda j: (0, first + j))


def scaled(values):
    scale = lax.rsqrt(jnp.mean(values * values, axis=-1, keepdims=True) + epsilon)
    return values * scale, scale


def norm_back(gradient_normalized, base, scale, gain):
    grad_base = gradient_normalized * gain
    return scale * (grad_base - base * jnp.mean(grad_base * base, axis=-1, keepdims=True))


def vmem():
    return pltpu.CompilerParams(vmem_limit_bytes=56 * MiB)


def smem():
    return pl.BlockSpec(memory_space=pltpu.SMEM)


def lay(parts, places_ref, target):
    rows = target.shape[0] // 16
    i = 0
    for part in parts:
        for k in range(part.shape[0]):
            target[pl.ds(pl.multiple_of(places_ref[i] * rows, 16), rows), :] = part[k]
            i += 1


def in_projection(values, pieces, places):
    tokens, width = values.shape
    rows = tokens // 4
    outer = pieces[0].shape[2]
    inner = outer - lane

    def body(places_ref, v_ref, *refs):
        parts, (normed_ref, out_ref, small_ref, w_ref) = refs[:-4], refs[-4:]

        @pl.when(pl.program_id(0) == 0)
        def _():
            lay(parts, places_ref, w_ref)
            small_ref[...] = w_ref[:, inner:].astype(f32).T[:8, :]

        base, _ = scaled(v_ref[...].astype(f32))
        normed_ref[...] = (base * small_ref[:1, :]).astype(bf16)
        out_ref[...] = matmul(normed_ref[...], w_ref[:, :inner])

    by_rows = pl.BlockSpec((rows, width), lambda j: (j, 0))
    return pl.pallas_call(
        body,
        grid=(4,),
        in_specs=[smem(), by_rows] + [whole(p.shape) for p in pieces],
        out_specs=[by_rows, pl.BlockSpec((rows, inner), lambda j: (j, 0)), whole((8, width)), whole((width, outer))],
        out_shape=[
            jax.ShapeDtypeStruct((tokens, width), bf16),
            jax.ShapeDtypeStruct((tokens, inner), f32),
            jax.ShapeDtypeStruct((8, width), f32),
            jax.ShapeDtypeStruct((width, outer), bf16),
        ],
        compiler_params=vmem(),
    )(places, values, *pieces)


def out_projection(place, values, mixed, weight, gain):
    rows, width = values.shape
    part = width // 4

    def body(z_ref, v_ref, *refs):
        blocks, (w_ref, gain_ref, mixed_ref, middle_ref, normed_ref) = refs[:4], refs[4:]
        for d in range(4):
            at = pl.multiple_of(lax.rem(z_ref[0] + d, 4) * part, lane)
            mixed_ref[:, pl.ds(at, part)] = blocks[d][...]
        middle = v_ref[...].astype(f32) + matmul(mixed_ref[...], w_ref[...])
        middle_ref[...] = middle
        base, _ = scaled(middle)
        normed_ref[...] = (base * gain_ref[...]).astype(bf16)

    return pl.pallas_call(
        body,
        in_specs=[smem(), whole(values.shape)] + [whole((rows, part))] * 4 + [whole(weight.shape), whole(gain.shape)],
        out_specs=[whole((rows, width))] * 3,
        out_shape=[jax.ShapeDtypeStruct((rows, width), t) for t in (bf16, f32, bf16)],
        grid=(1,),
        compiler_params=vmem(),
    )(place, values, *mixed, weight, gain)


def summed(parts):
    total = parts[0][...].astype(f32)
    for part in parts[1:]:
        total = total + part[...].astype(f32)
    return total


def middle_back(place, parts, middle, gain, grad_result, weight):
    rows, width = middle.shape
    part = width // 4

    def body(z_ref, middle_ref, gain_ref, result_ref, w_ref, *refs):
        parts, (grad_ref, mixer_ref, *mixed_refs) = refs[:4], refs[4:]
        base, scale = scaled(middle_ref[...])
        grad = result_ref[...] + norm_back(summed(parts), base, scale, gain_ref[...])
        grad_ref[...] = grad
        mixer_ref[...] = grad.astype(bf16)
        for d in range(4):
            at = pl.ds(pl.multiple_of(lax.rem(z_ref[0] + d, 4) * part, lane), part)
            mixed_refs[d][...] = matmul_right_t(mixer_ref[...], w_ref[at, :]).astype(bf16)

    return pl.pallas_call(
        body,
        in_specs=[smem()] + [whole(a.shape) for a in (middle, gain, grad_result, weight, *parts)],
        out_specs=[whole((rows, width))] * 2 + [whole((rows, part))] * 4,
        out_shape=[jax.ShapeDtypeStruct((rows, width), t) for t in (f32, bf16)]
        + [jax.ShapeDtypeStruct((rows, part), bf16)] * 4,
        grid=(1,),
        compiler_params=vmem(),
    )(place, middle, gain, grad_result, weight, *parts)


def token_back(parts, tokens, gain, grad_middle):
    rows, width = tokens.shape

    def body(tokens_ref, gain_ref, middle_ref, *refs):
        base, scale = scaled(tokens_ref[...].astype(f32))
        refs[4][...] = middle_ref[...] + norm_back(summed(refs[:4]), base, scale, gain_ref[...])

    return pl.pallas_call(
        body,
        in_specs=[whole(a.shape) for a in (tokens, gain, grad_middle, *parts)],
        out_specs=whole((rows, width)),
        out_shape=jax.ShapeDtypeStruct((rows, width), f32),
        grid=(1,),
        compiler_params=vmem(),
    )(tokens, gain, grad_middle, *parts)


def in_projection_back(grad_mixed, heads, conv_out, triple, taps, weight):
    blocks, rows, part = grad_mixed.shape
    inner = 3 * part
    width = weight.shape[0]

    def body(grad_ref, heads_ref, conv_ref, triple_ref, taps_ref, w_ref, out_ref, parts_ref):
        grad_mixed = grad_ref[0].astype(f32)
        grad_conv = grad_mixed * triple_ref[:, part : 2 * part]
        row = lax.broadcasted_iota(jnp.int32, (rows, part), 0)
        first, second = heads_ref[0, 0:1, :], heads_ref[0, 1:2, :]
        one = jnp.where(row == rows - 1, first, pltpu.roll(grad_conv, rows - 1, 0))
        two = pltpu.roll(grad_conv, rows - 2, 0)
        two = jnp.where(row == rows - 2, first, jnp.where(row == rows - 1, second, two))
        grad = taps_ref[2:3, :] * grad_conv + taps_ref[1:2, :] * one + taps_ref[0:1, :] * two
        out_ref[:, :part] = (grad * triple_ref[:, 2 * part : inner]).astype(bf16)
        out_ref[:, part : 2 * part] = (grad_mixed * conv_ref[0]).astype(bf16)
        out_ref[:, 2 * part : inner] = (grad * triple_ref[:, :part]).astype(bf16)
        out_ref[:, inner:] = jnp.zeros((rows, lane), bf16)
        parts_ref[0] = matmul_right_t(out_ref[:, :inner], w_ref[:, :inner]).astype(bf16)

    def block(*shape):
        return pl.BlockSpec((1, *shape), lambda j: (j, 0, 0))

    return pl.pallas_call(
        body,
        grid=(blocks,),
        in_specs=[
            block(rows, part),
            block(2, part),
            block(rows, part),
            pl.BlockSpec((rows, inner), lambda j: (j, 0)),
            whole(taps.shape),
            whole(weight.shape),
        ],
        out_specs=[pl.BlockSpec((rows, inner + lane), lambda j: (j, 0)), block(rows, width)],
        out_shape=[
            jax.ShapeDtypeStruct((blocks * rows, inner + lane), bf16),
            jax.ShapeDtypeStruct((blocks, rows, width), bf16),
        ],
        compiler_params=vmem(),
    )(grad_mixed, heads, conv_out, triple, taps, weight)


def turn(left, places, turned, moved):
    turned[...] = left[...].T
    rows = turned.shape[0] // 16
    for i in range(16):
        at = pl.multiple_of(places[i] * rows, 16)
        moved[i * rows : (i + 1) * rows, :] = turned[pl.ds(at, rows), :]


def mixer_gradients(normed, grad_triple, places, extra, grad_mixer, mixed):
    tokens, width = normed.shape
    inner, part = grad_triple.shape[1], mixed.shape[1]
    half = width // 2

    def body(places_ref, normed_ref, triple_ref, extra_ref, mixer_ref, mixed_ref, send_ref, keep_ref, turned, moved):
        for left, right, at in (
            (normed_ref, triple_ref, slice(0, inner)),
            (mixer_ref, mixed_ref, slice(inner, inner + part)),
        ):
            turn(left, places_ref, turned, moved)
            for ref, start in ((keep_ref, 0), (send_ref, half)):
                ref[:, at] = matmul(moved[start : start + half, :], right[...]).astype(bf16)
        rows = width // 16
        for i in range(16):
            ref = keep_ref if i < 8 else send_ref
            at = pl.multiple_of(places_ref[i] * rows, 16)
            ref[i % 8 * rows : (i % 8 + 1) * rows, inner - lane : inner] = extra_ref[pl.ds(at, rows), :]

    return pl.pallas_call(
        body,
        grid=(1,),
        in_specs=[smem()] + [whole(a.shape) for a in (normed, grad_triple, extra, grad_mixer, mixed)],
        out_specs=[whole((half, inner + part))] * 2,
        out_shape=[jax.ShapeDtypeStruct((half, inner + part), bf16)] * 2,
        scratch_shapes=[pltpu.VMEM((width, tokens), bf16)] * 2,
        compiler_params=vmem(),
    )(places, normed, grad_triple, extra, grad_mixer, mixed)


def feed_forward(normed, grads, weights, places, down):
    tokens, width = normed.shape
    padded = down.shape[0]
    chunk = 256
    steps = padded // chunk
    pieces = len(weights)
    rows = tokens // 4

    def body(places_ref, n_ref, g_ref, *refs):
        gates, ups = refs[:pieces], refs[pieces : 2 * pieces]
        d_ref, active_ref, pair_ref, *out_refs, gate_w, up_w, all_w, all_grads = refs[2 * pieces :]
        step = pl.program_id(0)
        lay(gates, places_ref, gate_w)
        lay(ups, places_ref, up_w)
        here = pl.ds(pl.multiple_of(step * chunk, chunk), chunk)
        later = pl.ds(pl.multiple_of(padded + step * chunk, chunk), chunk)
        all_w[:, here] = gate_w[...]
        all_w[:, later] = up_w[...]
        gate = matmul(n_ref[...], gate_w[...])
        up = matmul(n_ref[...], up_w[...])
        grad = matmul_right_t(g_ref[...], d_ref[...])
        sig = jax.nn.sigmoid(gate)
        silu = gate * sig
        active_ref[...] = (silu * up).astype(bf16)
        gg = (grad * up * sig * (1.0 + gate * (1.0 - sig))).astype(bf16)
        gu = (grad * silu).astype(bf16)
        pair_ref[0] = gg
        pair_ref[1] = gu
        all_grads[:, here] = gg
        all_grads[:, later] = gu

        @pl.when(step == steps - 1)
        def _():
            for at in range(0, width, width // 4):
                at = slice(at, at + width // 4)
                total = matmul_right_t(all_grads[...], all_w[at, :]).astype(bf16)
                for d, out_ref in enumerate(out_refs):
                    out_ref[:, at] = total[d * rows : (d + 1) * rows, :]

    def block(part, first):
        return pl.BlockSpec((*part.shape[:2], chunk), lambda j: (0, 0, first + j))

    return pl.pallas_call(
        body,
        grid=(steps,),
        in_specs=[smem(), whole((tokens, width)), whole((tokens, width))]
        + [block(part, 0) for part in weights]
        + [block(part, steps) for part in weights]
        + [pl.BlockSpec((chunk, width), lambda j: (j, 0))],
        out_specs=[
            columns(tokens, chunk),
            pl.BlockSpec((2, tokens, chunk), lambda j: (0, 0, j)),
        ]
        + [whole((rows, width))] * 4,
        out_shape=[
            jax.ShapeDtypeStruct((tokens, padded), bf16),
            jax.ShapeDtypeStruct((2, tokens, padded), bf16),
        ]
        + [jax.ShapeDtypeStruct((rows, width), bf16)] * 4,
        scratch_shapes=[pltpu.VMEM((width, chunk), bf16)] * 2
        + [pltpu.VMEM((width, 2 * padded), bf16), pltpu.VMEM((tokens, 2 * padded), bf16)],
        compiler_params=vmem(),
    )(places, normed, grads, *weights, *weights, down)


def feed_forward_weights(normed, grads, active, pair, places, place, down):
    tokens, width = normed.shape
    padded = down.shape[0]
    half = width // 2
    rows = tokens // 4
    chunk = 256
    steps = padded // chunk

    def body(places_ref, z_ref, n_ref, g_ref, a_ref, pair_ref, d_ref, *refs):
        send_ref, keep_ref, down_send_ref, down_keep_ref, out_ref, done_ref, turned, moved, down_w, total = refs
        step = pl.program_id(0)

        @pl.when(step == 0)
        def _():
            turn(n_ref, places_ref, turned, moved)
            total[...] = jnp.zeros_like(total)

        for i in range(2):
            keep_ref[i] = matmul(moved[:half, :], pair_ref[i]).astype(bf16)
            send_ref[i] = matmul(moved[half:, :], pair_ref[i]).astype(bf16)
        a = a_ref[...]
        here = pl.ds(pl.multiple_of(step * chunk, chunk), chunk)
        down_w[here, :] = lax.dot_general(a, g_ref[...], (((0,), (0,)), ((), ())), preferred_element_type=f32).astype(bf16)
        total[...] += matmul(a, d_ref[...])

        @pl.when(step == steps - 1)
        def _():
            done_ref[...] = jnp.zeros_like(done_ref)
            for d in range(4):
                out_ref[pl.ds(lax.rem(z_ref[0] + 4 - d, 4), 1)] = total[d * rows : (d + 1) * rows, :].astype(bf16)[None]
            for i in range(16):
                ref = down_keep_ref if i < 8 else down_send_ref
                at = pl.multiple_of(places_ref[i] * wide, 16)
                ref[i % 8 * wide : (i % 8 + 1) * wide, :] = down_w[pl.ds(at, wide), :]

    def both(rows):
        return pl.BlockSpec((2, rows, chunk), lambda j: (0, 0, j))

    return pl.pallas_call(
        body,
        grid=(steps,),
        in_specs=[
            smem(),
            smem(),
            whole((tokens, width)),
            whole((tokens, width)),
            columns(tokens, chunk),
            both(tokens),
            pl.BlockSpec((chunk, width), lambda j: (j, 0)),
        ],
        out_specs=[both(half)] * 2
        + [whole((padded // 2, width))] * 2
        + [whole((4, rows, width)), whole((8, lane))],
        out_shape=[jax.ShapeDtypeStruct((2, half, padded), bf16)] * 2
        + [jax.ShapeDtypeStruct((padded // 2, width), bf16)] * 2
        + [jax.ShapeDtypeStruct((4, rows, width), bf16), jax.ShapeDtypeStruct((8, lane), f32)],
        scratch_shapes=[pltpu.VMEM((width, tokens), bf16)] * 2
        + [pltpu.VMEM((padded, width), bf16), pltpu.VMEM((tokens, width), f32)],
        compiler_params=vmem(),
    )(places, place, normed, grads, active, pair, down)


def pick_hidden(place, gate, up):
    rows, hidden = gate.shape
    owned = hidden // 16
    share = owned // 4
    padded = 16 * wide

    def body(z_ref, gate_ref, up_ref, out_ref):
        for z in range(4):

            @pl.when(z_ref[0] == z)
            def _():
                for i, ref in enumerate((gate_ref, up_ref)):
                    parts = []
                    for d in range(16):
                        start = owned * d + share * z
                        parts += [ref[:, start : start + share], jnp.zeros((rows, wide - share), bf16)]
                    out_ref[:, padded * i : padded * (i + 1)] = jnp.concatenate(parts, axis=1)

    return pl.pallas_call(
        body,
        in_specs=[smem(), whole(gate.shape), whole(up.shape)],
        out_specs=whole((rows, 2 * padded)),
        out_shape=jax.ShapeDtypeStruct((rows, 2 * padded), bf16),
        grid=(1,),
        compiler_params=vmem(),
    )(place, gate, up)


def spread_hidden(parts, gate, up):
    rows, hidden = gate.shape
    owned = hidden // 16
    share = owned // 4
    padded = 16 * wide
    chunk = 16

    def body(parts_ref, gate_ref, up_ref, grad_gate_ref, grad_up_ref, sums_ref):
        sums = None
        for i, (w_ref, out_ref) in enumerate(((gate_ref, grad_gate_ref), (up_ref, grad_up_ref))):
            blocks = [parts_ref[z, i].astype(f32) for z in range(4)]
            pieces = [blocks[z][:, wide * d : wide * d + share] for d in range(16) for z in range(4)]
            out = jnp.concatenate(pieces, axis=1)
            out_ref[...] = out
            term = jnp.sum(out * w_ref[...].astype(f32), axis=1, keepdims=True)
            sums = term if sums is None else sums + term
        sums_ref[...] = jnp.broadcast_to(sums, (chunk, lane))

    by_rows = pl.BlockSpec((chunk, hidden), lambda j: (j, 0))
    return pl.pallas_call(
        body,
        grid=(rows // chunk,),
        in_specs=[pl.BlockSpec((4, 2, chunk, padded), lambda j: (0, 0, j, 0)), by_rows, by_rows],
        out_specs=[by_rows, by_rows, pl.BlockSpec((chunk, lane), lambda j: (j, 0))],
        out_shape=[jax.ShapeDtypeStruct((rows, hidden), f32)] * 2 + [jax.ShapeDtypeStruct((rows, lane), f32)],
        compiler_params=vmem(),
    )(parts, gate, up)


def local(
    tokens,
    lengths,
    cotangent,
    gain_one,
    in_weight,
    conv_weight,
    out_weight,
    gain_two,
    gate_weight,
    up_weight,
    down_weight,
):
    rows, width = tokens.shape[1:]
    z, xh, y, xl, core = (lax.axis_index(name) for name in ("z", "xh", "y", "xl", "core"))
    own_rows = width // 16
    part = width // 4
    quarter = width // 4
    hidden_rows = down_weight.shape[0]
    share = hidden_rows // 4
    padded = 16 * wide

    position = (z * 2 + xh) * rows + jnp.arange(rows, dtype=jnp.int32)
    valid = (position < lengths[0]).astype(f32)[:, None]
    tokens_here = tokens[0]
    grad_result = valid * cotangent[0].astype(f32)
    grad_branch = grad_result.astype(bf16)

    index = jnp.arange(16, dtype=jnp.int32)
    places = ((index % 4) * 2 + (index // 4 % 2 ^ xl)) * 2 + (index // 8 ^ core)
    places_behind = (((y - index) % 4) * 2 + (index // 4 % 2 ^ xl)) * 2 + (index // 8 ^ core)

    def gather(value):
        return lax.all_gather(value, owners, axis=0, tiled=True)

    def both_cores(parts):
        return parts + [shift(part, "core", 1) for part in parts]

    def send_back(parts):
        return [shift(parts[d], "z", -d) for d in range(4)]

    with scope("in_y"):
        small = jnp.concatenate([gain_one[:, None], gain_two[:, None], conv_weight.T], axis=1)
        in_slice = [lax.dynamic_slice_in_dim(in_weight, i * width + z * part, part, axis=1) for i in range(3)]
        in_y = gather_now(jnp.concatenate(in_slice + [jnp.pad(small, ((0, 0), (0, lane - 5)))], axis=1), "y")
    with scope("tokens_z"):
        token_parts = along(jnp.stack([tokens_here, grad_branch]), "z")
    with scope("out_all"):
        out_all = gather(out_weight)
    with scope("in_x"):
        in_pieces = both_cores([in_y, *across_x(*by_half(in_y))])
    with scope("pair_y"):
        pair_slice = pick_hidden(z[None], gate_weight, up_weight)
        pair_y = gather_now(tie(pair_slice, in_y), "y")
    with scope("down_all"):
        down_slice = lax.dynamic_slice_in_dim(down_weight, z * share, share, axis=0)
        down_all = gather(jnp.pad(down_slice, ((0, wide - share), (0, 0))))

    with scope("triple"):
        value_all = jnp.concatenate([block[0] for block in token_parts], axis=0)
        grad_all = jnp.concatenate([block[1] for block in token_parts], axis=0)
        normed, triple, small, in_all = in_projection(value_all, in_pieces, places)
        gain_first, gain_second = small[0:1], small[1:2]
        taps = lax.dynamic_slice_in_dim(small[2:5], z * part, part, axis=1)
        triple_blocks = triple.reshape(4, rows, 3 * part)
        output_gate = triple_blocks[..., part : 2 * part]
        gated_in = triple_blocks[..., :part] * triple_blocks[..., 2 * part :]
        tails = shift(gated_in[:, rows - 2 :], "xh", 1)
    with scope("conv"):
        block_z = (z - jnp.arange(4)) % 4
        first = ((block_z == 0) & (xh == 0))[:, None, None]
        tails = jnp.where(xh == 1, tails, jnp.roll(tails, -1, axis=0))
        tails = jnp.where(first, 0.0, tails)
        extended = jnp.concatenate([tails, gated_in], axis=1)
        conv_out = taps[0] * extended[:, :rows] + taps[1] * extended[:, 1 : rows + 1] + taps[2] * extended[:, 2:]
        mixed = (output_gate * conv_out).astype(bf16)
        pair_y = tie(pair_y, mixed)
        mixed_blocks = mixed
        mixed = send_back(mixed)
    with scope("pair_x"):
        pair_x = across_x(*by_half(pair_y))
        pair_y_other = shift(pair_y, "core", 1)
    with scope("out_projection"):
        mixed = [tie(mixed[0], pair_y_other), *mixed[1:]]
        mixed, middle, normed_two = out_projection(z[None], tokens_here, mixed, out_all, gain_second)
    with scope("normed_z"):
        normed_all = gather_now(normed_two, "z")
        normed_all = [lax.dynamic_index_in_dim(normed_all, (z - d) % 4, axis=0, keepdims=False) for d in range(4)]
        normed_all = jnp.concatenate(normed_all, axis=0)
    with scope("pair_core"):
        pair_x = [tie(part, normed_two) for part in pair_x]
        pair_pieces = [pair_y, *pair_x, pair_y_other, *(shift(part, "core", 1) for part in pair_x)]

    with scope("feed_forward"):
        active, grad_pair, *grad_parts = feed_forward(normed_all, grad_all, pair_pieces, places, down_all)
        grad_parts = send_back(grad_parts)
    with scope("feed_forward_weights"):
        pair_send, pair_keep, down_send, down_keep, branch, done = feed_forward_weights(
            normed_all, grad_all, active, grad_pair, places, z[None], down_all
        )
    with scope("middle_back"):
        grad_middle, grad_mixer, *grad_mixed = middle_back(
            z[None], [tie(grad_parts[0], done), *grad_parts[1:]], middle, gain_second, grad_result, out_all
        )
        grad_mixed = jnp.stack([shift(grad_mixed[d], "z", d) for d in range(4)])
    with scope("pair_wcore"):
        pair_core = shift(tie(pair_send, grad_mixer), "core", 1)
    with scope("down_wcore"):
        down_core = shift(tie(down_send, grad_mixer), "core", 1)
    with scope("heads"):
        heads = shift(grad_mixed[:, :2].astype(f32) * output_gate[:, :2], "xh", 1)
    with scope("branch"):
        branch = lax.psum_scatter(tie(branch, heads), "z", scatter_dimension=0, tiled=False)
    with scope("triple_back"):
        heads = jnp.where(xh == 0, heads, jnp.roll(heads, 1, axis=0))
        last = ((block_z == 3) & (xh == 1))[:, None, None]
        heads = jnp.where(last, 0.0, heads)
        grad_triple, grad_parts = in_projection_back(grad_mixed, heads, conv_out, triple, taps, in_all)
        grad_first = send_back(grad_parts)
    with scope("pair_wx"):
        pair_core = tie(pair_core, grad_parts)
        pair_x = (pair_keep[:, quarter:].astype(f32) + pair_core[:, quarter:].astype(f32)).astype(bf16)
        pair_gate, pair_up = pair_x[0], pair_x[1]
        pair_x = across_x(pair_gate, pair_up)
    with scope("down_wx"):
        eighth = padded // 4
        down_core = tie(down_core, pair_gate)
        down_x = (down_keep[eighth:].astype(f32) + down_core[eighth:].astype(f32)).astype(bf16)
        down_upper, down_lower = by_half(down_x)
        down_x = across_x(down_upper, down_lower)
    with scope("out_z"):
        mixer_all = gather_now(tie(grad_mixer, grad_parts), "z")
    with scope("taps_back"):
        grad_conv = grad_mixed.astype(f32) * output_gate
        grad_taps = jnp.stack([jnp.sum(grad_conv * extended[:, k : k + rows], axis=(0, 1)) for k in range(3)])
        grad_taps = jnp.pad(grad_taps, ((0, lane - 3), (0, 0))).T.astype(bf16)
        grad_taps = lax.dynamic_update_slice(jnp.zeros((width, lane), bf16), grad_taps, (z * part, 0))
    with scope("pair_wy"):
        mine = pair_keep[:, :quarter].astype(f32) + pair_core[:, :quarter].astype(f32)
        mine = (mine + jnp.stack([tie(pair_x[0], grad_parts, branch), pair_x[1]]).astype(f32)).astype(bf16)
        pair_mine = mine.reshape(2, 4, own_rows, padded).transpose(1, 0, 2, 3)
        pair_w = exchange(pair_mine, "y")
    with scope("in_w"):
        mixer_all = [lax.dynamic_index_in_dim(mixer_all, (z - d) % 4, axis=0, keepdims=False) for d in range(4)]
        in_send, in_keep = mixer_gradients(
            tie(normed, pair_mine),
            grad_triple,
            places_behind,
            grad_taps,
            jnp.concatenate(mixer_all, axis=0),
            mixed_blocks.reshape(4 * rows, part),
        )
        in_core = shift(in_send, "core", 1)
    with scope("token_back"):
        grad_tokens = token_back([tie(grad_first[0], in_send), *grad_first[1:]], tokens_here, gain_first, grad_middle)
    with scope("in_wx"):
        in_x = (in_keep[quarter:].astype(f32) + in_core[quarter:].astype(f32)).astype(bf16)
        in_upper, in_lower = by_half(in_x)
        in_x = across_x(in_upper, in_lower)
    with scope("in_wy"):
        mine = in_keep[:quarter].astype(f32) + in_core[:quarter].astype(f32)
        mine = mine + jnp.concatenate([tie(in_x[0], grad_tokens), in_x[1]], axis=0).astype(f32)
        in_mine = mine.astype(bf16).reshape(4, own_rows, -1)
    with scope("pair_wxh"):
        pair_w = jnp.sum(tie(pair_w, grad_tokens, in_mine).astype(f32), axis=0).astype(bf16)
        pair_partner = add_partner(pair_w)
    with scope("in_wy"):
        in_blocks = tie(in_mine, pair_w)
        in_w = in_blocks[0].astype(f32)
        for d in (1, 2, 3):
            in_w = in_w + shift(in_blocks[d], "y", -d).astype(f32)
        in_w = in_w.astype(bf16)
        in_partner = add_partner(in_w)
    with scope("down_wy"):
        down_mine = down_keep[:eighth].astype(f32) + down_core[:eighth].astype(f32)
        down_mine = down_mine + jnp.concatenate([tie(down_x[0], pair_w), down_x[1]], axis=0).astype(f32)
        down_mine = down_mine.astype(bf16).reshape(4, wide, width)
        down_w = lax.psum_scatter(down_mine, "y", scatter_dimension=0, tiled=False)
    with scope("pair_wz"):
        pair_z = gather_now(pair_partner, "z")
    with scope("in_wz"):
        in_w = gather_now(tie(in_partner, pair_z), "z")
    with scope("down_wz"):
        down_w = in_order(along(tie(add_partner(tie(down_w, pair_partner)), in_w), "z"), "z")
        grad_down_w = jnp.concatenate([piece[:share] for piece in down_w], axis=0).astype(f32)
    with scope("out_end"):
        out_w = jnp.concatenate([in_w[d, :, 3 * part + lane :] for d in range(4)], axis=1).T
        out_w = lax.all_to_all(out_w.reshape(16, own_rows, own_rows), owners, 0, 0, tiled=True)
        grad_out_w = out_w.transpose(1, 0, 2).reshape(own_rows, width).astype(f32)
    with scope("result"):
        result = valid * (middle + branch.astype(f32))
    with scope("in_end"):
        in_w = in_w[..., : 3 * part + lane].astype(f32)
        grad_in_w = jnp.concatenate([in_w[d, :, i * part : (i + 1) * part] for i in range(3) for d in range(4)], axis=1)
        grad_conv_w = jnp.sum(in_w[..., 3 * part :], axis=0)[:, :3].T
        grad_gain_one = jnp.sum(grad_in_w * in_weight.astype(f32), axis=1) / gain_one.astype(f32)
    with scope("pair_end"):
        grad_gate_w, grad_up_w, sums = spread_hidden(pair_z, gate_weight, up_weight)
        grad_gain_two = sums[:, 0] / gain_two.astype(f32)

    return (
        result.astype(bf16)[None],
        grad_tokens[None],
        grad_gain_one,
        grad_in_w,
        grad_conv_w,
        grad_out_w,
        grad_gain_two,
        grad_gate_w,
        grad_up_w,
        grad_down_w,
    )


def solution(mesh):
    fine = Mesh(mesh.devices.reshape(4, 2, 4, 2, 2), ("z", "xh", "y", "xl", "core"))
    by_rows = P(owners, None)
    sequences = P(owners, blocks, None)
    return jax.shard_map(
        local,
        mesh=fine,
        in_specs=(
            sequences,
            P(owners),
            sequences,
            P(owners),
            by_rows,
            P(None, owners),
            by_rows,
            P(owners),
            by_rows,
            by_rows,
            by_rows,
        ),
        out_specs=(
            sequences,
            sequences,
            P(owners),
            by_rows,
            P(None, owners),
            by_rows,
            P(owners),
            by_rows,
            by_rows,
            by_rows,
        ),
        check_vma=False,
    )
```

```python
import jax
import jax.numpy as jnp
from jax import lax
from jax.experimental import pallas as pl
from jax.experimental.pallas import tpu as pltpu
from jax.sharding import Mesh
from jax.sharding import PartitionSpec as P

epsilon = 1e-05
bf16 = jnp.bfloat16
f32 = jnp.float32
ring = ("xh", "xl")
owners = ("y", "xl", "core")
blocks = ("z", "xh")
lane = 128
MiB = 1024 * 1024
scope = jax.named_scope
wide = 112


def shift(value, axis, distance):
    if distance == 0:
        return value
    size = lax.axis_size(axis)
    return lax.ppermute(value, axis, [(i, (i + distance) % size) for i in range(size)])


def matmul(left, right):
    return jnp.dot(left, right, preferred_element_type=f32)


def matmul_right_t(left, right):
    return lax.dot_general(left, right, (((1,), (1,)), ((), ())), preferred_element_type=f32)


def exchange(value, axis):
    return lax.all_to_all(value, axis, 0, 0, tiled=True)


def gather_now(value, axis):
    return exchange(jnp.broadcast_to(value[None], (4,) + value.shape), axis)


def in_order(parts, axis):
    place = lax.axis_index(axis)
    stacked = jnp.stack(parts)
    return [lax.dynamic_index_in_dim(stacked, (place - i) % 4, axis=0, keepdims=False) for i in range(4)]


def along(value, axis):
    return [value] + [shift(value, axis, d) for d in (1, 2, 3)]


def across_x(upper, lower):
    return shift(upper, ring, 1), shift(lower, ring, -1)


def by_half(rows):
    half = rows.shape[0] // 2
    return rows[:half], rows[half:]


def add_partner(mine):
    return (mine.astype(f32) + shift(mine, "xh", 1).astype(f32)).astype(bf16)


def sum_y(mine):
    return jnp.sum(exchange(mine, "y").astype(f32), axis=0).astype(bf16)


def corner(value):
    return value[(0,) * (value.ndim - 2)][:16, :lane]


def tie(value, *others):
    others = [corner(other) for other in others]
    return pl.pallas_call(
        lambda *refs: None,
        out_shape=jax.ShapeDtypeStruct(value.shape, value.dtype),
        in_specs=[pl.BlockSpec(memory_space=pltpu.HBM)] * (1 + len(others)),
        out_specs=pl.BlockSpec(memory_space=pltpu.HBM),
        input_output_aliases={0: 0},
        compiler_params=pltpu.CompilerParams(vmem_limit_bytes=128 * 1024),
        cost_estimate=pl.CostEstimate(flops=0, bytes_accessed=0, transcendentals=0),
    )(value, *others)


def whole(shape):
    return pl.BlockSpec(shape, lambda *at: (0,) * len(shape))


def columns(rows, chunk, first=0):
    return pl.BlockSpec((rows, chunk), lambda j: (0, first + j))


def scaled(values):
    scale = lax.rsqrt(jnp.mean(values * values, axis=-1, keepdims=True) + epsilon)
    return values * scale, scale


def norm_back(gradient_normalized, base, scale, gain):
    grad_base = gradient_normalized * gain
    return scale * (grad_base - base * jnp.mean(grad_base * base, axis=-1, keepdims=True))


def vmem():
    return pltpu.CompilerParams(vmem_limit_bytes=56 * MiB)


def smem():
    return pl.BlockSpec(memory_space=pltpu.SMEM)


def lay(parts, places_ref, target):
    rows = target.shape[0] // 16
    i = 0
    for part in parts:
        for k in range(part.shape[0]):
            target[pl.ds(pl.multiple_of(places_ref[i] * rows, 16), rows), :] = part[k]
            i += 1


def in_projection(values, pieces, places):
    tokens, width = values.shape
    rows = tokens // 4
    outer = pieces[0].shape[2]
    inner = outer - lane

    def body(places_ref, v_ref, *refs):
        parts, (normed_ref, out_ref, small_ref, w_ref) = refs[:-4], refs[-4:]

        @pl.when(pl.program_id(0) == 0)
        def _():
            lay(parts, places_ref, w_ref)
            small_ref[...] = w_ref[:, inner:].astype(f32).T[:8, :]

        base, _ = scaled(v_ref[...].astype(f32))
        normed_ref[...] = (base * small_ref[:1, :]).astype(bf16)
        out_ref[...] = matmul(normed_ref[...], w_ref[:, :inner])

    by_rows = pl.BlockSpec((rows, width), lambda j: (j, 0))
    return pl.pallas_call(
        body,
        grid=(4,),
        in_specs=[smem(), by_rows] + [whole(p.shape) for p in pieces],
        out_specs=[by_rows, pl.BlockSpec((rows, inner), lambda j: (j, 0)), whole((8, width)), whole((width, outer))],
        out_shape=[
            jax.ShapeDtypeStruct((tokens, width), bf16),
            jax.ShapeDtypeStruct((tokens, inner), f32),
            jax.ShapeDtypeStruct((8, width), f32),
            jax.ShapeDtypeStruct((width, outer), bf16),
        ],
        compiler_params=vmem(),
    )(places, values, *pieces)


def out_projection(place, values, mixed, weight, gain):
    rows, width = values.shape
    part = width // 4

    def body(z_ref, v_ref, *refs):
        blocks, (w_ref, gain_ref, mixed_ref, middle_ref, normed_ref) = refs[:4], refs[4:]
        for d in range(4):
            at = pl.multiple_of(lax.rem(z_ref[0] + d, 4) * part, lane)
            mixed_ref[:, pl.ds(at, part)] = blocks[d][...]
        middle = v_ref[...].astype(f32) + matmul(mixed_ref[...], w_ref[...])
        middle_ref[...] = middle
        base, _ = scaled(middle)
        normed_ref[...] = (base * gain_ref[...]).astype(bf16)

    return pl.pallas_call(
        body,
        in_specs=[smem(), whole(values.shape)] + [whole((rows, part))] * 4 + [whole(weight.shape), whole(gain.shape)],
        out_specs=[whole((rows, width))] * 3,
        out_shape=[jax.ShapeDtypeStruct((rows, width), t) for t in (bf16, f32, bf16)],
        grid=(1,),
        compiler_params=vmem(),
    )(place, values, *mixed, weight, gain)


def summed(parts):
    total = parts[0][...].astype(f32)
    for part in parts[1:]:
        total = total + part[...].astype(f32)
    return total


def middle_back(place, parts, middle, gain, grad_result, weight):
    rows, width = middle.shape
    part = width // 4

    def body(z_ref, middle_ref, gain_ref, result_ref, w_ref, *refs):
        parts, (grad_ref, mixer_ref, *mixed_refs) = refs[:4], refs[4:]
        base, scale = scaled(middle_ref[...])
        grad = result_ref[...] + norm_back(summed(parts), base, scale, gain_ref[...])
        grad_ref[...] = grad
        mixer_ref[...] = grad.astype(bf16)
        for d in range(4):
            at = pl.ds(pl.multiple_of(lax.rem(z_ref[0] + d, 4) * part, lane), part)
            mixed_refs[d][...] = matmul_right_t(mixer_ref[...], w_ref[at, :]).astype(bf16)

    return pl.pallas_call(
        body,
        in_specs=[smem()] + [whole(a.shape) for a in (middle, gain, grad_result, weight, *parts)],
        out_specs=[whole((rows, width))] * 2 + [whole((rows, part))] * 4,
        out_shape=[jax.ShapeDtypeStruct((rows, width), t) for t in (f32, bf16)]
        + [jax.ShapeDtypeStruct((rows, part), bf16)] * 4,
        grid=(1,),
        compiler_params=vmem(),
    )(place, middle, gain, grad_result, weight, *parts)


def token_back(parts, tokens, gain, grad_middle):
    rows, width = tokens.shape

    def body(tokens_ref, gain_ref, middle_ref, *refs):
        base, scale = scaled(tokens_ref[...].astype(f32))
        refs[4][...] = middle_ref[...] + norm_back(summed(refs[:4]), base, scale, gain_ref[...])

    return pl.pallas_call(
        body,
        in_specs=[whole(a.shape) for a in (tokens, gain, grad_middle, *parts)],
        out_specs=whole((rows, width)),
        out_shape=jax.ShapeDtypeStruct((rows, width), f32),
        grid=(1,),
        compiler_params=vmem(),
    )(tokens, gain, grad_middle, *parts)


def in_projection_back(grad_mixed, heads, conv_out, triple, taps, weight):
    blocks, rows, part = grad_mixed.shape
    inner = 3 * part
    width = weight.shape[0]

    def body(grad_ref, heads_ref, conv_ref, triple_ref, taps_ref, w_ref, out_ref, parts_ref):
        grad_mixed = grad_ref[0].astype(f32)
        grad_conv = grad_mixed * triple_ref[:, part : 2 * part]
        row = lax.broadcasted_iota(jnp.int32, (rows, part), 0)
        first, second = heads_ref[0, 0:1, :], heads_ref[0, 1:2, :]
        one = jnp.where(row == rows - 1, first, pltpu.roll(grad_conv, rows - 1, 0))
        two = pltpu.roll(grad_conv, rows - 2, 0)
        two = jnp.where(row == rows - 2, first, jnp.where(row == rows - 1, second, two))
        grad = taps_ref[2:3, :] * grad_conv + taps_ref[1:2, :] * one + taps_ref[0:1, :] * two
        out_ref[:, :part] = (grad * triple_ref[:, 2 * part : inner]).astype(bf16)
        out_ref[:, part : 2 * part] = (grad_mixed * conv_ref[0]).astype(bf16)
        out_ref[:, 2 * part : inner] = (grad * triple_ref[:, :part]).astype(bf16)
        out_ref[:, inner:] = jnp.zeros((rows, lane), bf16)
        parts_ref[0] = matmul_right_t(out_ref[:, :inner], w_ref[:, :inner]).astype(bf16)

    def block(*shape):
        return pl.BlockSpec((1, *shape), lambda j: (j, 0, 0))

    return pl.pallas_call(
        body,
        grid=(blocks,),
        in_specs=[
            block(rows, part),
            block(2, part),
            block(rows, part),
            pl.BlockSpec((rows, inner), lambda j: (j, 0)),
            whole(taps.shape),
            whole(weight.shape),
        ],
        out_specs=[pl.BlockSpec((rows, inner + lane), lambda j: (j, 0)), block(rows, width)],
        out_shape=[
            jax.ShapeDtypeStruct((blocks * rows, inner + lane), bf16),
            jax.ShapeDtypeStruct((blocks, rows, width), bf16),
        ],
        compiler_params=vmem(),
    )(grad_mixed, heads, conv_out, triple, taps, weight)


def turn(left, places, turned, moved):
    turned[...] = left[...].T
    rows = turned.shape[0] // 16
    for i in range(16):
        at = pl.multiple_of(places[i] * rows, 16)
        moved[i * rows : (i + 1) * rows, :] = turned[pl.ds(at, rows), :]


def mixer_gradients(normed, grad_triple, places, extra, grad_mixer, mixed):
    tokens, width = normed.shape
    inner, part = grad_triple.shape[1], mixed.shape[1]
    half = width // 2

    def body(places_ref, normed_ref, triple_ref, extra_ref, mixer_ref, mixed_ref, send_ref, keep_ref, turned, moved):
        for left, right, at in (
            (normed_ref, triple_ref, slice(0, inner)),
            (mixer_ref, mixed_ref, slice(inner, inner + part)),
        ):
            turn(left, places_ref, turned, moved)
            for ref, start in ((keep_ref, 0), (send_ref, half)):
                ref[:, at] = matmul(moved[start : start + half, :], right[...]).astype(bf16)
        rows = width // 16
        for i in range(16):
            ref = keep_ref if i < 8 else send_ref
            at = pl.multiple_of(places_ref[i] * rows, 16)
            ref[i % 8 * rows : (i % 8 + 1) * rows, inner - lane : inner] = extra_ref[pl.ds(at, rows), :]

    return pl.pallas_call(
        body,
        grid=(1,),
        in_specs=[smem()] + [whole(a.shape) for a in (normed, grad_triple, extra, grad_mixer, mixed)],
        out_specs=[whole((half, inner + part))] * 2,
        out_shape=[jax.ShapeDtypeStruct((half, inner + part), bf16)] * 2,
        scratch_shapes=[pltpu.VMEM((width, tokens), bf16)] * 2,
        compiler_params=vmem(),
    )(places, normed, grad_triple, extra, grad_mixer, mixed)


def feed_forward(normed, grads, weights, places, down):
    tokens, width = normed.shape
    padded = down.shape[0]
    chunk = 256
    steps = padded // chunk
    pieces = len(weights)
    rows = tokens // 4

    def body(places_ref, n_ref, g_ref, *refs):
        gates, ups = refs[:pieces], refs[pieces : 2 * pieces]
        d_ref, active_ref, pair_ref, *out_refs, gate_w, up_w, all_w, all_grads = refs[2 * pieces :]
        step = pl.program_id(0)
        lay(gates, places_ref, gate_w)
        lay(ups, places_ref, up_w)
        here = pl.ds(pl.multiple_of(step * chunk, chunk), chunk)
        later = pl.ds(pl.multiple_of(padded + step * chunk, chunk), chunk)
        all_w[:, here] = gate_w[...]
        all_w[:, later] = up_w[...]
        gate = matmul(n_ref[...], gate_w[...])
        up = matmul(n_ref[...], up_w[...])
        grad = matmul_right_t(g_ref[...], d_ref[...])
        sig = jax.nn.sigmoid(gate)
        silu = gate * sig
        active_ref[...] = (silu * up).astype(bf16)
        gg = (grad * up * sig * (1.0 + gate * (1.0 - sig))).astype(bf16)
        gu = (grad * silu).astype(bf16)
        pair_ref[0] = gg
        pair_ref[1] = gu
        all_grads[:, here] = gg
        all_grads[:, later] = gu

        @pl.when(step == steps - 1)
        def _():
            for at in range(0, width, width // 4):
                at = slice(at, at + width // 4)
                total = matmul_right_t(all_grads[...], all_w[at, :]).astype(bf16)
                for d, out_ref in enumerate(out_refs):
                    out_ref[:, at] = total[d * rows : (d + 1) * rows, :]

    def block(part, first):
        return pl.BlockSpec((*part.shape[:2], chunk), lambda j: (0, 0, first + j))

    return pl.pallas_call(
        body,
        grid=(steps,),
        in_specs=[smem(), whole((tokens, width)), whole((tokens, width))]
        + [block(part, 0) for part in weights]
        + [block(part, steps) for part in weights]
        + [pl.BlockSpec((chunk, width), lambda j: (j, 0))],
        out_specs=[
            columns(tokens, chunk),
            pl.BlockSpec((2, tokens, chunk), lambda j: (0, 0, j)),
        ]
        + [whole((rows, width))] * 4,
        out_shape=[
            jax.ShapeDtypeStruct((tokens, padded), bf16),
            jax.ShapeDtypeStruct((2, tokens, padded), bf16),
        ]
        + [jax.ShapeDtypeStruct((rows, width), bf16)] * 4,
        scratch_shapes=[pltpu.VMEM((width, chunk), bf16)] * 2
        + [pltpu.VMEM((width, 2 * padded), bf16), pltpu.VMEM((tokens, 2 * padded), bf16)],
        compiler_params=vmem(),
    )(places, normed, grads, *weights, *weights, down)


def feed_forward_weights(normed, grads, active, pair, places, place, down):
    tokens, width = normed.shape
    padded = down.shape[0]
    half = width // 2
    rows = tokens // 4
    chunk = 256
    steps = padded // chunk

    def body(places_ref, z_ref, n_ref, g_ref, a_ref, pair_ref, d_ref, *refs):
        send_ref, keep_ref, down_send_ref, down_keep_ref, out_ref, done_ref, turned, moved, down_w, total = refs
        step = pl.program_id(0)

        @pl.when(step == 0)
        def _():
            turn(n_ref, places_ref, turned, moved)
            total[...] = jnp.zeros_like(total)

        for i in range(2):
            keep_ref[i] = matmul(moved[:half, :], pair_ref[i]).astype(bf16)
            send_ref[i] = matmul(moved[half:, :], pair_ref[i]).astype(bf16)
        a = a_ref[...]
        here = pl.ds(pl.multiple_of(step * chunk, chunk), chunk)
        down_w[here, :] = lax.dot_general(a, g_ref[...], (((0,), (0,)), ((), ())), preferred_element_type=f32).astype(bf16)
        total[...] += matmul(a, d_ref[...])

        @pl.when(step == steps - 1)
        def _():
            done_ref[...] = jnp.zeros_like(done_ref)
            for d in range(4):
                out_ref[pl.ds(lax.rem(z_ref[0] + 4 - d, 4), 1)] = total[d * rows : (d + 1) * rows, :].astype(bf16)[None]
            for i in range(16):
                ref = down_keep_ref if i < 8 else down_send_ref
                at = pl.multiple_of(places_ref[i] * wide, 16)
                ref[i % 8 * wide : (i % 8 + 1) * wide, :] = down_w[pl.ds(at, wide), :]

    def both(rows):
        return pl.BlockSpec((2, rows, chunk), lambda j: (0, 0, j))

    return pl.pallas_call(
        body,
        grid=(steps,),
        in_specs=[
            smem(),
            smem(),
            whole((tokens, width)),
            whole((tokens, width)),
            columns(tokens, chunk),
            both(tokens),
            pl.BlockSpec((chunk, width), lambda j: (j, 0)),
        ],
        out_specs=[both(half)] * 2
        + [whole((padded // 2, width))] * 2
        + [whole((4, rows, width)), whole((8, lane))],
        out_shape=[jax.ShapeDtypeStruct((2, half, padded), bf16)] * 2
        + [jax.ShapeDtypeStruct((padded // 2, width), bf16)] * 2
        + [jax.ShapeDtypeStruct((4, rows, width), bf16), jax.ShapeDtypeStruct((8, lane), f32)],
        scratch_shapes=[pltpu.VMEM((width, tokens), bf16)] * 2
        + [pltpu.VMEM((padded, width), bf16), pltpu.VMEM((tokens, width), f32)],
        compiler_params=vmem(),
    )(places, place, normed, grads, active, pair, down)


def pick_hidden(place, gate, up):
    rows, hidden = gate.shape
    owned = hidden // 16
    share = owned // 4
    padded = 16 * wide

    def body(z_ref, gate_ref, up_ref, out_ref):
        for z in range(4):

            @pl.when(z_ref[0] == z)
            def _():
                for i, ref in enumerate((gate_ref, up_ref)):
                    parts = []
                    for d in range(16):
                        start = owned * d + share * z
                        parts += [ref[:, start : start + share], jnp.zeros((rows, wide - share), bf16)]
                    out_ref[:, padded * i : padded * (i + 1)] = jnp.concatenate(parts, axis=1)

    return pl.pallas_call(
        body,
        in_specs=[smem(), whole(gate.shape), whole(up.shape)],
        out_specs=whole((rows, 2 * padded)),
        out_shape=jax.ShapeDtypeStruct((rows, 2 * padded), bf16),
        grid=(1,),
        compiler_params=vmem(),
    )(place, gate, up)


def spread_hidden(parts, gate, up):
    rows, hidden = gate.shape
    owned = hidden // 16
    share = owned // 4
    padded = 16 * wide
    chunk = 16

    def body(parts_ref, gate_ref, up_ref, grad_gate_ref, grad_up_ref, sums_ref):
        sums = None
        for i, (w_ref, out_ref) in enumerate(((gate_ref, grad_gate_ref), (up_ref, grad_up_ref))):
            blocks = [parts_ref[z, i].astype(f32) for z in range(4)]
            pieces = [blocks[z][:, wide * d : wide * d + share] for d in range(16) for z in range(4)]
            out = jnp.concatenate(pieces, axis=1)
            out_ref[...] = out
            term = jnp.sum(out * w_ref[...].astype(f32), axis=1, keepdims=True)
            sums = term if sums is None else sums + term
        sums_ref[...] = jnp.broadcast_to(sums, (chunk, lane))

    by_rows = pl.BlockSpec((chunk, hidden), lambda j: (j, 0))
    return pl.pallas_call(
        body,
        grid=(rows // chunk,),
        in_specs=[pl.BlockSpec((4, 2, chunk, padded), lambda j: (0, 0, j, 0)), by_rows, by_rows],
        out_specs=[by_rows, by_rows, pl.BlockSpec((chunk, lane), lambda j: (j, 0))],
        out_shape=[jax.ShapeDtypeStruct((rows, hidden), f32)] * 2 + [jax.ShapeDtypeStruct((rows, lane), f32)],
        compiler_params=vmem(),
    )(parts, gate, up)


def local(
    tokens,
    lengths,
    cotangent,
    gain_one,
    in_weight,
    conv_weight,
    out_weight,
    gain_two,
    gate_weight,
    up_weight,
    down_weight,
):
    rows, width = tokens.shape[1:]
    z, xh, y, xl, core = (lax.axis_index(name) for name in ("z", "xh", "y", "xl", "core"))
    own_rows = width // 16
    part = width // 4
    quarter = width // 4
    hidden_rows = down_weight.shape[0]
    share = hidden_rows // 4
    padded = 16 * wide

    position = (z * 2 + xh) * rows + jnp.arange(rows, dtype=jnp.int32)
    valid = (position < lengths[0]).astype(f32)[:, None]
    tokens_here = tokens[0]
    grad_result = valid * cotangent[0].astype(f32)
    grad_branch = grad_result.astype(bf16)

    index = jnp.arange(16, dtype=jnp.int32)
    places = ((index % 4) * 2 + (index // 4 % 2 ^ xl)) * 2 + (index // 8 ^ core)
    places_behind = (((y - index) % 4) * 2 + (index // 4 % 2 ^ xl)) * 2 + (index // 8 ^ core)

    def gather(value):
        return lax.all_gather(value, owners, axis=0, tiled=True)

    def both_cores(parts):
        return parts + [shift(part, "core", 1) for part in parts]

    def send_back(parts):
        return [shift(parts[d], "z", -d) for d in range(4)]

    with scope("in_y"):
        small = jnp.concatenate([gain_one[:, None], gain_two[:, None], conv_weight.T], axis=1)
        in_slice = [lax.dynamic_slice_in_dim(in_weight, i * width + z * part, part, axis=1) for i in range(3)]
        in_y = gather_now(jnp.concatenate(in_slice + [jnp.pad(small, ((0, 0), (0, lane - 5)))], axis=1), "y")
    with scope("tokens_z"):
        token_parts = along(jnp.stack([tokens_here, grad_branch]), "z")
    with scope("out_all"):
        out_all = gather(out_weight)
    with scope("in_x"):
        in_pieces = both_cores([in_y, *across_x(*by_half(in_y))])
    with scope("pair_y"):
        pair_slice = pick_hidden(z[None], gate_weight, up_weight)
        pair_y = gather_now(tie(pair_slice, in_y), "y")
    with scope("down_all"):
        down_slice = lax.dynamic_slice_in_dim(down_weight, z * share, share, axis=0)
        down_all = gather(jnp.pad(down_slice, ((0, wide - share), (0, 0))))

    with scope("triple"):
        value_all = jnp.concatenate([block[0] for block in token_parts], axis=0)
        grad_all = jnp.concatenate([block[1] for block in token_parts], axis=0)
        normed, triple, small, in_all = in_projection(value_all, in_pieces, places)
        gain_first, gain_second = small[0:1], small[1:2]
        taps = lax.dynamic_slice_in_dim(small[2:5], z * part, part, axis=1)
        triple_blocks = triple.reshape(4, rows, 3 * part)
        output_gate = triple_blocks[..., part : 2 * part]
        gated_in = triple_blocks[..., :part] * triple_blocks[..., 2 * part :]
        tails = shift(gated_in[:, rows - 2 :], "xh", 1)
    with scope("conv"):
        block_z = (z - jnp.arange(4)) % 4
        first = ((block_z == 0) & (xh == 0))[:, None, None]
        tails = jnp.where(xh == 1, tails, jnp.roll(tails, -1, axis=0))
        tails = jnp.where(first, 0.0, tails)
        extended = jnp.concatenate([tails, gated_in], axis=1)
        conv_out = taps[0] * extended[:, :rows] + taps[1] * extended[:, 1 : rows + 1] + taps[2] * extended[:, 2:]
        mixed = (output_gate * conv_out).astype(bf16)
        pair_y = tie(pair_y, mixed)
        mixed_blocks = mixed
        mixed = send_back(mixed)
    with scope("pair_x"):
        pair_x = across_x(*by_half(pair_y))
        pair_y_other = shift(pair_y, "core", 1)
    with scope("out_projection"):
        mixed = [tie(mixed[0], pair_y_other), tie(mixed[1], grad_all), *mixed[2:]]
        mixed, middle, normed_two = out_projection(z[None], tokens_here, mixed, out_all, gain_second)
    with scope("normed_z"):
        normed_all = gather_now(normed_two, "z")
        normed_all = [lax.dynamic_index_in_dim(normed_all, (z - d) % 4, axis=0, keepdims=False) for d in range(4)]
        normed_all = jnp.concatenate(normed_all, axis=0)
    with scope("pair_core"):
        pair_x = [tie(part, normed_two) for part in pair_x]
        pair_pieces = [pair_y, *pair_x, pair_y_other, *(shift(part, "core", 1) for part in pair_x)]

    with scope("feed_forward"):
        active, grad_pair, *grad_parts = feed_forward(normed_all, grad_all, pair_pieces, places, down_all)
        grad_parts = send_back(grad_parts)
    with scope("feed_forward_weights"):
        pair_send, pair_keep, down_send, down_keep, branch, done = feed_forward_weights(
            normed_all, grad_all, active, grad_pair, places, z[None], down_all
        )
    with scope("middle_back"):
        grad_middle, grad_mixer, *grad_mixed = middle_back(
            z[None], [tie(grad_parts[0], done), *grad_parts[1:]], middle, gain_second, grad_result, out_all
        )
        grad_mixed = jnp.stack([shift(grad_mixed[d], "z", d) for d in range(4)])
    with scope("pair_wcore"):
        pair_core = shift(tie(pair_send, grad_mixer), "core", 1)
    with scope("down_wcore"):
        down_core = shift(tie(down_send, grad_mixer), "core", 1)
    with scope("heads"):
        heads = shift(grad_mixed[:, :2].astype(f32) * output_gate[:, :2], "xh", 1)
    with scope("branch"):
        branch = lax.psum_scatter(tie(branch, heads), "z", scatter_dimension=0, tiled=False)
    with scope("triple_back"):
        heads = jnp.where(xh == 0, heads, jnp.roll(heads, 1, axis=0))
        last = ((block_z == 3) & (xh == 1))[:, None, None]
        heads = jnp.where(last, 0.0, heads)
        grad_triple, grad_parts = in_projection_back(grad_mixed, heads, conv_out, triple, taps, in_all)
        grad_first = send_back(grad_parts)
    with scope("pair_wx"):
        pair_core = tie(pair_core, grad_parts)
        pair_x = (pair_keep[:, quarter:].astype(f32) + pair_core[:, quarter:].astype(f32)).astype(bf16)
        pair_gate, pair_up = pair_x[0], pair_x[1]
        pair_x = across_x(pair_gate, pair_up)
    with scope("down_wx"):
        eighth = padded // 4
        down_core = tie(down_core, pair_gate)
        down_x = (down_keep[eighth:].astype(f32) + down_core[eighth:].astype(f32)).astype(bf16)
        down_upper, down_lower = by_half(down_x)
        down_x = across_x(down_upper, down_lower)
    with scope("out_z"):
        mixer_all = gather_now(tie(grad_mixer, pair_gate), "z")
    with scope("taps_back"):
        grad_conv = grad_mixed.astype(f32) * output_gate
        grad_taps = jnp.stack([jnp.sum(grad_conv * extended[:, k : k + rows], axis=(0, 1)) for k in range(3)])
        grad_taps = jnp.pad(grad_taps, ((0, lane - 3), (0, 0))).T.astype(bf16)
        grad_taps = lax.dynamic_update_slice(jnp.zeros((width, lane), bf16), grad_taps, (z * part, 0))
    with scope("pair_wy"):
        mine = pair_keep[:, :quarter].astype(f32) + pair_core[:, :quarter].astype(f32)
        mine = (mine + jnp.stack([tie(pair_x[0], grad_parts, branch), pair_x[1]]).astype(f32)).astype(bf16)
        pair_mine = mine.reshape(2, 4, own_rows, padded).transpose(1, 0, 2, 3)
        pair_w = exchange(pair_mine, "y")
    with scope("in_w"):
        mixer_all = [lax.dynamic_index_in_dim(mixer_all, (z - d) % 4, axis=0, keepdims=False) for d in range(4)]
        in_send, in_keep = mixer_gradients(
            tie(normed, pair_mine),
            grad_triple,
            places_behind,
            grad_taps,
            jnp.concatenate(mixer_all, axis=0),
            mixed_blocks.reshape(4 * rows, part),
        )
        in_core = shift(in_send, "core", 1)
    with scope("token_back"):
        grad_tokens = token_back([tie(grad_first[0], in_send), *grad_first[1:]], tokens_here, gain_first, grad_middle)
    with scope("in_wx"):
        in_x = (in_keep[quarter:].astype(f32) + in_core[quarter:].astype(f32)).astype(bf16)
        in_upper, in_lower = by_half(in_x)
        in_x = across_x(in_upper, in_lower)
    with scope("in_wy"):
        mine = in_keep[:quarter].astype(f32) + in_core[:quarter].astype(f32)
        mine = mine + jnp.concatenate([tie(in_x[0], grad_tokens), in_x[1]], axis=0).astype(f32)
        in_mine = mine.astype(bf16).reshape(4, own_rows, -1)
    with scope("pair_wxh"):
        pair_w = jnp.sum(tie(pair_w, grad_tokens, in_mine).astype(f32), axis=0).astype(bf16)
        pair_partner = add_partner(pair_w)
    with scope("in_wy"):
        in_blocks = tie(in_mine, pair_w)
        in_w = in_blocks[0].astype(f32)
        for d in (1, 2, 3):
            in_w = in_w + shift(in_blocks[d], "y", -d).astype(f32)
        in_w = in_w.astype(bf16)
        in_partner = add_partner(in_w)
    with scope("down_wy"):
        down_mine = down_keep[:eighth].astype(f32) + down_core[:eighth].astype(f32)
        down_mine = down_mine + jnp.concatenate([tie(down_x[0], pair_w), down_x[1]], axis=0).astype(f32)
        down_mine = down_mine.astype(bf16).reshape(4, wide, width)
        down_w = lax.psum_scatter(down_mine, "y", scatter_dimension=0, tiled=False)
    with scope("pair_wz"):
        pair_z = gather_now(pair_partner, "z")
    with scope("in_wz"):
        in_w = gather_now(tie(in_partner, pair_z), "z")
    with scope("down_wz"):
        down_w = in_order(along(tie(add_partner(tie(down_w, pair_partner)), in_w), "z"), "z")
        grad_down_w = jnp.concatenate([piece[:share] for piece in down_w], axis=0).astype(f32)
    with scope("out_end"):
        out_w = jnp.concatenate([in_w[d, :, 3 * part + lane :] for d in range(4)], axis=1).T
        out_w = lax.all_to_all(out_w.reshape(16, own_rows, own_rows), owners, 0, 0, tiled=True)
        grad_out_w = out_w.transpose(1, 0, 2).reshape(own_rows, width).astype(f32)
    with scope("result"):
        result = valid * (middle + branch.astype(f32))
    with scope("in_end"):
        in_w = in_w[..., : 3 * part + lane].astype(f32)
        grad_in_w = jnp.concatenate([in_w[d, :, i * part : (i + 1) * part] for i in range(3) for d in range(4)], axis=1)
        grad_conv_w = jnp.sum(in_w[..., 3 * part :], axis=0)[:, :3].T
        grad_gain_one = jnp.sum(grad_in_w * in_weight.astype(f32), axis=1) / gain_one.astype(f32)
    with scope("pair_end"):
        grad_gate_w, grad_up_w, sums = spread_hidden(pair_z, gate_weight, up_weight)
        grad_gain_two = sums[:, 0] / gain_two.astype(f32)

    return (
        result.astype(bf16)[None],
        grad_tokens[None],
        grad_gain_one,
        grad_in_w,
        grad_conv_w,
        grad_out_w,
        grad_gain_two,
        grad_gate_w,
        grad_up_w,
        grad_down_w,
    )


def solution(mesh):
    fine = Mesh(mesh.devices.reshape(4, 2, 4, 2, 2), ("z", "xh", "y", "xl", "core"))
    by_rows = P(owners, None)
    sequences = P(owners, blocks, None)
    return jax.shard_map(
        local,
        mesh=fine,
        in_specs=(
            sequences,
            P(owners),
            sequences,
            P(owners),
            by_rows,
            P(None, owners),
            by_rows,
            P(owners),
            by_rows,
            by_rows,
            by_rows,
        ),
        out_specs=(
            sequences,
            sequences,
            P(owners),
            by_rows,
            P(None, owners),
            by_rows,
            P(owners),
            by_rows,
            by_rows,
            by_rows,
        ),
        check_vma=False,
    )
```
